32 devices in a mesh: seq: 8 (over z, y), head: 4 (over x, core).
Axes of the slice: x: 2, y: 2, z: 4, core: 2. Of those that a mesh axis runs over, the one named last changes fastest.
Arguments:
- queries: bfloat16 [1024, 4096], P('seq', 'head'), may hold values from -6 to 6
- keys: bfloat16 [1024, 4096], P('seq', 'head'), may hold values from -6 to 6
- values: bfloat16 [1024, 4096], P('seq', 'head'), may hold values from -6 to 6
- hidden: bfloat16 [1024, 2048], P('seq', 'head'), may hold values from -6 to 6
- gate_weight: bfloat16 [2048, 128], P('head'), may hold values from -0.125 to 0.125
- level_slot: int32 [4], replicated, may hold values from 0 to 3, each once
- out_grad: bfloat16 [1024, 4096], P('seq', 'head'), may hold values from -6 to 6
Outputs:
- mixed: bfloat16 [1024, 4096], P('seq', 'head')
- grad_queries: bfloat16 [1024, 4096], P('seq', 'head')
- grad_keys: bfloat16 [1024, 4096], P('seq', 'head')
- grad_values: bfloat16 [1024, 4096], P('seq', 'head')
- grad_hidden: bfloat16 [1024, 2048], P('seq', 'head')
The draws below stay inside these ranges and needn't reach their ends.
Inputs may be any that keep to these rules, and one draw needn't show every extreme that they name: `level_slot`: each column index of a head's block appears once.
All inputs are finite; a program needn't handle non-finite values.
Results may differ from the reference program's by a relative error of at most 0.01.
Values may be sent and summed in bfloat16 or wider, within the bound.
A program may use at most 64 MiB of HBM per device.

```python
import jax
import jax.numpy as jnp
from jax import lax

HEADS = 32
DK = 128
D = 2048
SPAN = 128
TOKENS = 1024
LEVELS = 4


def steps_of(key, dims, pieces, low, top_value):
    def one(dim, shards_of):
        heights = jax.random.uniform(jax.random.fold_in(jax.random.fold_in(key, 6), dim), (shards_of,), jnp.float32, low / len(pieces), top_value / len(pieces))
        return jnp.repeat(jnp.exp(heights), dims[dim] // shards_of).reshape((-1,) + (1,) * (len(dims) - dim - 1))

    level = one(*pieces[0])
    for cut in pieces[1:]:
        level = level * one(*cut)
    return level


def bell_draw(stream_key, dims, deviation, reach, cuts=(), kind=jnp.bfloat16):
    result = jax.random.normal(stream_key, dims, jnp.float32) * deviation
    if len(cuts) > 0:
        result = steps_of(stream_key, dims, cuts, -0.22, 0.18) * result
    return jnp.clip(result, min=-reach, max=reach).astype(kind)


def setup_inputs(seed: int = 0) -> dict:
    key_list = jax.random.split(jax.random.key(seed), 8)
    queries = bell_draw(key_list[0], (TOKENS, HEADS * DK), 1.0, 6.0, ((0, 8), (1, 4)))
    keys = bell_draw(key_list[1], (TOKENS, HEADS * DK), 1.0, 6.0, ((0, 8), (1, 4)))
    values = bell_draw(key_list[2], (TOKENS, HEADS * DK), 1.0, 6.0, ((0, 8), (1, 4)))
    hidden = bell_draw(key_list[3], (TOKENS, D), 1.0, 6.0, ((0, 8), (1, 4)))
    gate_weight = bell_draw(key_list[4], (D, HEADS * LEVELS), D ** -0.5, 0.125, ((0, 4),))
    level_slot = jax.random.permutation(key_list[5], LEVELS).astype(jnp.int32)
    out_grad = bell_draw(key_list[6], (TOKENS, HEADS * DK), 1.0, 6.0, ((0, 8), (1, 4)))
    return dict(queries=queries, keys=keys, values=values, hidden=hidden, gate_weight=gate_weight, level_slot=level_slot, out_grad=out_grad)


HIGH = lax.Precision.HIGHEST


def rounded(array):
    return lax.optimization_barrier(array.astype(jnp.bfloat16)).astype(jnp.float32)


def mix_head(items):
    query, key_part, value, grad, weight = items
    query = query.astype(jnp.float32)
    key_part = key_part.astype(jnp.float32)
    value = value.astype(jnp.float32)
    grad = grad.astype(jnp.float32)
    count = query.shape[0]
    position = jnp.arange(SPAN)
    causal = (position[:, None] >= position[None, :]).astype(jnp.float32)
    scores = jnp.einsum('ncd,nsd->ncs', query, key_part, precision=HIGH)
    attend = rounded(scores * causal / SPAN)
    intra = jnp.einsum('ncs,nse->nce', attend, value, precision=HIGH)
    states = jnp.einsum('ncd,nce->nde', key_part, value, precision=HIGH)
    mixed = weight[:, :, 0:1] * intra
    weight_grads = [jnp.sum(grad * intra, -1)]
    grad_query = jnp.zeros_like(query)
    state_grad = jnp.zeros_like(states)
    span_ids = jnp.arange(count, dtype=jnp.int32)
    for depth in range(1, LEVELS):
        shift_bits = depth - 1
        width = 1 << shift_bits
        blocks = states.reshape(count // width, width, DK, DK).sum(1)
        upper_bit = ((span_ids >> shift_bits) & 1)[:, None, None]
        below = blocks[jnp.maximum((span_ids >> shift_bits) - 1, 0).astype(jnp.int32)]
        level_state = rounded(jnp.where(upper_bit == 1, below, 0.0) / float(width * SPAN))
        level_out = jnp.einsum('ncd,nde->nce', query, level_state, precision=HIGH)
        level_weight = weight[:, :, depth:depth + 1]
        mixed = mixed + level_weight * level_out
        weight_grads.append(jnp.sum(grad * level_out, -1))
        grad_query = grad_query + level_weight * jnp.einsum('nce,nde->ncd', grad, level_state, precision=HIGH)
        weighted = rounded(level_weight * grad)
        level_grad = jnp.einsum('ncd,nce->nde', query, weighted, precision=HIGH)
        grad_blocks = level_grad.reshape(count // width, width, DK, DK).sum(1)
        above = grad_blocks[jnp.minimum((span_ids >> shift_bits) + 1, count // width - 1).astype(jnp.int32)]
        state_grad = state_grad + jnp.where(upper_bit == 0, above, 0.0) / float(width * SPAN)
    state_grad = rounded(state_grad)
    weighted_first = rounded(weight[:, :, 0:1] * grad)
    grad_score = rounded(jnp.einsum('nce,nse->ncs', weighted_first, value, precision=HIGH) * causal / SPAN)
    grad_query = grad_query + jnp.einsum('ncs,nsd->ncd', grad_score, key_part, precision=HIGH)
    grad_key = jnp.einsum('ncs,ncd->nsd', grad_score, query, precision=HIGH) + jnp.einsum('nce,nde->ncd', value, state_grad, precision=HIGH)
    grad_value = jnp.einsum('ncs,nce->nse', attend, weighted_first, precision=HIGH) + jnp.einsum('ncd,nde->nce', key_part, state_grad, precision=HIGH)
    return mixed, grad_query, grad_key, grad_value, jnp.stack(weight_grads, -1)


def reference(queries, keys, values, hidden, gate_weight, level_slot, out_grad):
    tokens = queries.shape[0]
    count = tokens // SPAN
    logits = jnp.dot(hidden, gate_weight, preferred_element_type=jnp.float32).reshape(tokens, HEADS, LEVELS)
    chosen = logits[:, :, level_slot.astype(jnp.int32)]
    weight = jax.nn.softplus(chosen)

    def split(array):
        return jnp.transpose(array.reshape(count, SPAN, HEADS, -1), (2, 0, 1, 3))

    def join(array):
        return jnp.transpose(array, (1, 2, 0, 3)).reshape(tokens, -1)

    mixed, grad_query, grad_key, grad_value, weight_grad = lax.map(
        mix_head, (split(queries), split(keys), split(values), split(out_grad), split(weight)))
    weight_grad = join(weight_grad).reshape(tokens, HEADS, LEVELS)
    chosen_grad = weight_grad * jax.nn.sigmoid(chosen)
    logit_grad = jnp.zeros_like(logits).at[:, :, level_slot.astype(jnp.int32)].set(chosen_grad)
    logit_grad = logit_grad.reshape(tokens, HEADS * LEVELS).astype(jnp.bfloat16)
    grad_hidden = jnp.dot(logit_grad, gate_weight.T, preferred_element_type=jnp.float32).astype(jnp.bfloat16)
    return (join(mixed).astype(jnp.bfloat16), join(grad_query).astype(jnp.bfloat16),
            join(grad_key).astype(jnp.bfloat16), join(grad_value).astype(jnp.bfloat16), grad_hidden)
```

```python
import functools

import jax
import jax.numpy as jnp
from jax import lax
from jax.experimental import pallas as pl
from jax.experimental.pallas import tpu as pltpu
from jax.sharding import PartitionSpec as P

DK = 128
MESH = pl.DeviceIdType.MESH
F32 = jnp.float32
BF16 = jnp.bfloat16
CHUNK_HEADS = 2


def dot(a, b, ca, cb):
    return lax.dot_general(a, b, (((ca,), (cb,)), ((), ())), preferred_element_type=F32)


def mix_kernel(
    seq_n, head_n,
    slot_ref, q_ref, k_ref, v_ref, hid_ref, gate_ref, g_ref,
    mixed_ref, gq_ref, gk_ref, gv_ref, ghid_ref,
    gatep, lp_send, lp_recv, lg_all,
    s_f32, s_bf, pair_recv, ls, h_send, r_send, r_recv, m_send, m_recv,
    intra, lev, lev1, gq_acc, gk_acc, gv_acc, wgt,
    lp_ss, lp_rs, lg_ss, lg_rs, pr_ss, pr_rs, up_ss, up_rs, dn_ss, dn_rs, m_ss, m_rs,
):
    tok = q_ref.shape[0]
    heads = q_ref.shape[1] // DK
    levels = lev.shape[0] + 2
    nb = levels - 2
    rows = heads * levels
    ch = min(CHUNK_HEADS, heads)
    chunks = heads // ch
    zn = seq_n // 2

    me = lax.axis_index("seq")
    hd = lax.axis_index("head")
    odd = me % 2
    z = me // 2
    pair = me + 1 - 2 * odd
    above = jnp.minimum(z + 1, zn - 1) * 2 + odd
    below = jnp.maximum(z - 1, 0) * 2 + odd
    is_top = z == zn - 1
    not_top = z < zn - 1
    not_low = z > 0
    bit = [(z // (1 << j)) % 2 for j in range(nb)]
    jstar = jnp.int32(nb)
    for j in reversed(range(nb)):
        jstar = jnp.where(bit[j] == 0, j, jstar)
    peers = [lax.rem(hd + d, head_n) for d in range(1, head_n)]

    barrier = pltpu.get_barrier_semaphore()
    pl.semaphore_signal(barrier, inc=1, device_id={"seq": pair}, device_id_type=MESH)
    for p in peers:
        pl.semaphore_signal(barrier, inc=1, device_id={"head": p}, device_id_type=MESH)

    @pl.when(not_top)
    def _():
        pl.semaphore_signal(barrier, inc=1, device_id={"seq": above}, device_id_type=MESH)

    @pl.when(not_low)
    def _():
        pl.semaphore_signal(barrier, inc=1, device_id={"seq": below}, device_id_type=MESH)

    def cs(k):
        return pl.ds(k * ch, ch)

    def copy(src, dst, ss, rs, where):
        return pltpu.make_async_remote_copy(
            src_ref=src, dst_ref=dst, send_sem=ss, recv_sem=rs, device_id=where, device_id_type=MESH
        )

    def lp_copy(d):
        return copy(
            lp_send.at[peers[d - 1]], lp_recv.at[d - 1], lp_ss.at[d - 1], lp_rs.at[d - 1],
            {"head": peers[d - 1]},
        )

    def lg_copy(d):
        return copy(
            lg_all.at[hd], lg_all.at[hd], lg_ss.at[d - 1], lg_rs.at[d - 1], {"head": peers[d - 1]}
        )

    def lg_wait(d):
        src = lax.rem(hd + head_n - d, head_n)
        copy(lg_all.at[src], lg_all.at[src], lg_ss.at[d - 1], lg_rs.at[d - 1], {"head": peers[d - 1]}).wait_recv()

    def pair_copy(k):
        return copy(s_bf.at[cs(k)], pair_recv.at[cs(k)], pr_ss.at[k], pr_rs.at[k], {"seq": pair})

    def up_copy(j, k):
        return copy(ls.at[j, cs(k)], ls.at[j, cs(k)], up_ss.at[j, k], up_rs.at[j, k], {"seq": above})

    def h_copy(k):
        j = jnp.minimum(jstar, nb - 1)
        return copy(h_send.at[cs(k)], ls.at[j, cs(k)], up_ss.at[j, k], up_rs.at[j, k], {"seq": above})

    def down_copy(j, k):
        return copy(r_send.at[j, cs(k)], r_recv.at[j, cs(k)], dn_ss.at[j, k], dn_rs.at[j, k], {"seq": below})

    def m_copy(k):
        return copy(m_send.at[cs(k)], m_recv.at[cs(k)], m_ss.at[k], m_rs.at[k], {"seq": pair})

    def hs(ref, h):
        return ref[:, h * DK:(h + 1) * DK]

    wide = head_n * rows
    r_from = lax.broadcasted_iota(jnp.int32, (wide, wide), 0)
    r_to = lax.broadcasted_iota(jnp.int32, (wide, wide), 1)
    in_dev = r_to % rows
    lev_of = in_dev // heads
    slot_of = jnp.zeros((wide, wide), jnp.int32)
    for l in range(levels):
        slot_of = jnp.where(lev_of == l, slot_ref[l], slot_of)
    target = (r_to // rows) * rows + (in_dev % heads) * levels + slot_of
    perm = jnp.where(r_from == target, 1.0, 0.0).astype(BF16)
    gatep[...] = dot(gate_ref[...], perm, 1, 0).astype(BF16)
    partial = dot(hid_ref[...], gatep[...], 1, 0).T
    for p in range(head_n):
        lp_send[p] = partial[p * rows:(p + 1) * rows, :]

    for h in range(ch):
        s = dot(hs(k_ref, h), hs(v_ref, h), 0, 0)
        s_f32[h] = s
        s_bf[h] = s.astype(BF16)

    for j in range(nb):
        @pl.when(bit[j] == 0)
        def _(j=j):
            ls[j] = jnp.zeros(ls.shape[1:], BF16)

    r_recv[nb] = jnp.zeros(r_recv.shape[1:], BF16)

    @pl.when(jnp.logical_and(is_top, odd == 0))
    def _():
        pair_recv[...] = jnp.zeros(pair_recv.shape, BF16)

    @pl.when(jnp.logical_and(is_top, odd == 1))
    def _():
        m_recv[...] = jnp.zeros(m_recv.shape, BF16)

    pl.semaphore_wait(
        barrier, head_n + jnp.where(not_top, 1, 0) + jnp.where(not_low, 1, 0)
    )
    for d in range(1, head_n):
        lp_copy(d).start()

    sends_s = jnp.logical_or(odd == 0, not_top)
    gets_s = jnp.logical_or(odd == 1, not_top)
    sends_m = jnp.logical_or(odd == 1, not_top)
    gets_m = jnp.logical_or(odd == 0, not_top)

    for k in range(chunks):
        if k > 0:
            for h in range(k * ch, (k + 1) * ch):
                s = dot(hs(k_ref, h), hs(v_ref, h), 0, 0)
                s_f32[h] = s
                s_bf[h] = s.astype(BF16)

        @pl.when(sends_s)
        def _(k=k):
            pair_copy(k).start()

    t_pos = lax.broadcasted_iota(jnp.int32, (tok, tok), 0)
    s_pos = lax.broadcasted_iota(jnp.int32, (tok, tok), 1)
    causal = jnp.where(t_pos >= s_pos, 1.0 / tok, 0.0)
    attend = {}
    for h in range(heads):
        a = (dot(hs(q_ref, h), hs(k_ref, h), 1, 1) * causal).astype(BF16)
        gv_acc[:, h * DK:(h + 1) * DK] = a.astype(F32)
        intra[:, h * DK:(h + 1) * DK] = dot(a, hs(v_ref, h), 1, 0)

    def f1(k):
        @pl.when(gets_s)
        def _():
            pair_copy(k).wait_recv()

        @pl.when(jnp.logical_and(not_top, jstar == 0))
        def _():
            h_send[cs(k)] = (s_f32[cs(k)] + pair_recv[cs(k)].astype(F32)).astype(BF16)
            h_copy(k).start()

    def f2(k):
        @pl.when(not_top)
        def _():
            for j in range(nb):
                @pl.when(bit[j] == 1)
                def _(j=j):
                    up_copy(j, k).wait_recv()

            @pl.when(jstar > 0)
            def _():
                total = s_f32[cs(k)] + pair_recv[cs(k)].astype(F32)
                for j in range(nb):
                    total = total + jnp.where(j < jstar, ls[j, cs(k)].astype(F32), 0.0)
                h_send[cs(k)] = total.astype(BF16)
                h_copy(k).start()

            for j in range(nb):
                @pl.when(jnp.logical_and(bit[j] == 1, j > jstar))
                def _(j=j):
                    up_copy(j, k).start()

    f1(0)

    mine = lp_send[hd]
    for d in range(1, head_n):
        lp_copy(d).wait_recv()
    for d in range(1, head_n):
        mine = mine + lp_recv[d - 1]
    soft = jnp.maximum(mine, 0.0) + jnp.log1p(jnp.exp(-jnp.abs(mine)))
    pad = jnp.zeros((DK - rows, tok), F32)
    soft_t = jnp.concatenate([soft, pad], 0).T if rows < DK else soft.T
    sig = jax.nn.sigmoid(mine)
    wgt[...] = soft_t

    def weight(l, h):
        return wgt[:, l * heads + h:l * heads + h + 1]

    def level_grads(k):
        for h in range(k * ch, (k + 1) * ch):
            gh = hs(g_ref, h).astype(F32)
            wgs = [(weight(l, h) * gh).astype(BF16) for l in range(1, levels)]
            grads = dot(hs(q_ref, h), jnp.concatenate(wgs, 1), 0, 0)
            lev1[h] = grads[:, :DK] * (1.0 / tok)
            for j in range(nb):
                lev[j, h] = grads[:, (j + 1) * DK:(j + 2) * DK] * (1.0 / (tok * 2 << j))

        @pl.when(is_top)
        def _():
            for j in reversed(range(nb)):
                r_send[j, cs(k)] = lev[j, cs(k)].astype(BF16)
                @pl.when(not_low)
                def _(j=j):
                    down_copy(j, k).start()

    def back(k):
        @pl.when(not_top)
        def _():
            for j in reversed(range(nb)):
                @pl.when(((z + 1) // (1 << j)) % 2 == 1)
                def _(j=j):
                    down_copy(j, k).wait_recv()

                @pl.when(bit[j] == 1)
                def _(j=j):
                    came = jnp.where(j < jstar, jstar, j)
                    r_send[j, cs(k)] = (lev[j, cs(k)] + r_recv[came, cs(k)].astype(F32)).astype(BF16)
                    down_copy(j, k).start()

        @pl.when(sends_m)
        def _():
            got = r_recv[jstar, cs(k)].astype(F32)
            own = jnp.where(odd == 1, 1.0, 0.0)
            m_send[cs(k)] = (got + own * lev1[cs(k)]).astype(BF16)
            m_copy(k).start()

    def span_grads(k):
        for h in range(k * ch, (k + 1) * ch):
            gh = hs(g_ref, h).astype(F32)
            w0 = (weight(0, h) * gh).astype(BF16)
            score = (dot(w0, hs(v_ref, h), 1, 1) * causal).astype(BF16)
            sl = slice(h * DK, (h + 1) * DK)
            a = gv_acc[:, sl].astype(BF16)
            gq_acc[:, sl] = dot(score, hs(k_ref, h), 1, 0)
            gk_acc[:, sl] = dot(score, hs(q_ref, h), 0, 0)
            gv_acc[:, sl] = dot(a, w0, 0, 0)

    for k in range(chunks):
        level_grads(k)
        if k + 1 < chunks:
            f1(k + 1)
        if k >= 1:
            f2(k - 1)
        if k >= 2:
            back(k - 2)
    f2(chunks - 1)
    for k in range(max(chunks - 2, 0), chunks):
        back(k)
        span_grads(k)
    for k in range(max(chunks - 2, 0)):
        span_grads(k)

    col = lax.broadcasted_iota(jnp.int32, (tok, DK), 1)
    scale1 = jnp.where(odd == 1, 1.0 / tok, 0.0)
    wg = jnp.zeros((tok, DK), F32)
    for k in range(chunks):
        @pl.when(is_top)
        def _(k=k):
            for j in range(nb):
                up_copy(j, k).wait_recv()

        for h in range(k * ch, (k + 1) * ch):
            sl = slice(h * DK, (h + 1) * DK)
            gh = hs(g_ref, h)
            gh32 = gh.astype(F32)
            part = intra[:, sl]
            out = weight(0, h) * part
            wg = jnp.where(col == h, jnp.sum(gh32 * part, 1, keepdims=True), wg)
            gq = gq_acc[:, sl]
            for l in range(1, levels):
                state = pair_recv[h] if l == 1 else ls[l - 2, h]
                scale = scale1 if l == 1 else 1.0 / (tok * (1 << (l - 1)))
                w = weight(l, h)
                lo = dot(hs(q_ref, h), state, 1, 0) * scale
                out = out + w * lo
                wg = jnp.where(col == l * heads + h, jnp.sum(gh32 * lo, 1, keepdims=True), wg)
                gq = gq + w * (dot(gh, state, 1, 1) * scale)
            mixed_ref[:, sl] = out.astype(BF16)
            gq_ref[:, sl] = gq.astype(BF16)

    lg_all[hd] = (wg.T[:rows, :] * sig).astype(BF16)
    for d in range(1, head_n):
        lg_copy(d).start()

    for k in range(chunks):
        @pl.when(gets_m)
        def _(k=k):
            m_copy(k).wait_recv()

        for h in range(k * ch, (k + 1) * ch):
            sl = slice(h * DK, (h + 1) * DK)
            sg = (r_recv[jstar, h].astype(F32) + m_recv[h].astype(F32)).astype(BF16)
            gk_ref[:, sl] = (gk_acc[:, sl] + dot(hs(v_ref, h), sg, 1, 1)).astype(BF16)
            gv_ref[:, sl] = (gv_acc[:, sl] + dot(hs(k_ref, h), sg, 1, 0)).astype(BF16)

    for d in range(1, head_n):
        lg_wait(d)
    every = jnp.concatenate([lg_all[p] for p in range(head_n)], 0)
    ghid_ref[...] = dot(every, gatep[...], 0, 1).astype(BF16)

    for d in range(1, head_n):
        lp_copy(d).wait_send()
        lg_copy(d).wait_send()
    for k in range(chunks):
        @pl.when(sends_s)
        def _(k=k):
            pair_copy(k).wait_send()

        @pl.when(sends_m)
        def _(k=k):
            m_copy(k).wait_send()

        for j in range(nb):
            @pl.when(jnp.logical_and(not_top, ((z + 1) // (1 << j)) % 2 == 1))
            def _(j=j, k=k):
                up_copy(j, k).wait_send()

            @pl.when(jnp.logical_and(not_low, bit[j] == 1))
            def _(j=j, k=k):
                down_copy(j, k).wait_send()


def local(seq_n, head_n, queries, keys, values, hidden, gate_weight, level_slot, out_grad):
    tok, width = queries.shape
    heads = width // DK
    levels = level_slot.shape[0]
    nb = levels - 2
    rows = heads * levels
    chunks = heads // min(CHUNK_HEADS, heads)
    feats = hidden.shape[1]
    wide = head_n * rows
    vm = pl.BlockSpec(memory_space=pltpu.VMEM)
    blk = (heads, DK, DK)
    sem = pltpu.SemaphoreType.DMA
    return pl.pallas_call(
        functools.partial(mix_kernel, seq_n, head_n),
        out_shape=[jax.ShapeDtypeStruct((tok, width), BF16)] * 4
        + [jax.ShapeDtypeStruct((tok, feats), BF16)],
        in_specs=[pl.BlockSpec(memory_space=pltpu.SMEM)] + [vm] * 6,
        out_specs=[vm] * 5,
        scratch_shapes=[
            pltpu.VMEM((feats, wide), BF16),
            pltpu.VMEM((head_n, rows, tok), F32),
            pltpu.VMEM((head_n - 1, rows, tok), F32),
            pltpu.VMEM((head_n, rows, tok), BF16),
            pltpu.VMEM(blk, F32),
            pltpu.VMEM(blk, BF16),
            pltpu.VMEM(blk, BF16),
            pltpu.VMEM((nb,) + blk, BF16),
            pltpu.VMEM(blk, BF16),
            pltpu.VMEM((nb,) + blk, BF16),
            pltpu.VMEM((nb + 1,) + blk, BF16),
            pltpu.VMEM(blk, BF16),
            pltpu.VMEM(blk, BF16),
            pltpu.VMEM((tok, width), F32),
            pltpu.VMEM((nb,) + blk, F32),
            pltpu.VMEM(blk, F32),
            pltpu.VMEM((tok, width), F32),
            pltpu.VMEM((tok, width), F32),
            pltpu.VMEM((tok, width), F32),
            pltpu.VMEM((tok, DK), F32),
            sem((head_n - 1,)), sem((head_n - 1,)),
            sem((head_n - 1,)), sem((head_n - 1,)),
            sem((chunks,)), sem((chunks,)),
            sem((nb, chunks)), sem((nb, chunks)),
            sem((nb, chunks)), sem((nb, chunks)),
            sem((chunks,)), sem((chunks,)),
        ],
        compiler_params=pltpu.CompilerParams(
            collective_id=0, has_side_effects=True, vmem_limit_bytes=48 << 20
        ),
    )(level_slot, queries, keys, values, hidden, gate_weight, out_grad)


def solution(mesh):
    both = P("seq", "head")
    return jax.shard_map(
        functools.partial(local, mesh.shape["seq"], mesh.shape["head"]),
        mesh=mesh,
        in_specs=(both, both, both, both, P("head", None), P(), both),
        out_specs=(both,) * 5,
        check_vma=False,
    )
```

```python
import functools

import jax
import jax.numpy as jnp
from jax import lax
from jax.experimental import pallas as pl
from jax.experimental.pallas import tpu as pltpu
from jax.sharding import PartitionSpec as P

DK = 128
MESH = pl.DeviceIdType.MESH
F32 = jnp.float32
BF16 = jnp.bfloat16
CHUNK_HEADS = 2
VMEM_ALL = (64 << 20) - (1 << 19)


def dot(a, b, ca, cb):
    return lax.dot_general(a, b, (((ca,), (cb,)), ((), ())), preferred_element_type=F32)


def mix_kernel(
    seq_n, head_n,
    slot_hbm, q_hbm, k_hbm, v_hbm, hid_hbm, gate_hbm, g_hbm,
    mixed_hbm, gq_hbm, gk_hbm, gv_hbm, ghid_hbm,
    slot_ref, q_ref, k_ref, v_ref, hid_ref, gate_ref, g_ref,
    mixed_ref, gq_ref, gk_ref, gv_ref, ghid_ref,
    gatep, lp_send, lp_recv, lg_all,
    s_f32, s_bf, pair_recv, ls, h_send, r_send, r_recv, m_send, m_recv,
    intra, lev, lev1, att_t, score, score_t, w_all, w0g, wlg,
    in_sem, out_sem, hid_sem,
    lp_ss, lp_rs, lg_ss, lg_rs, pr_ss, pr_rs, up_ss, up_rs, dn_ss, dn_rs, m_ss, m_rs,
):
    tok = q_ref.shape[0]
    heads = q_ref.shape[1] // DK
    levels = lev.shape[0] + 2
    nb = levels - 2
    rows = heads * levels
    ch = min(CHUNK_HEADS, heads)
    chunks = heads // ch
    zn = seq_n // 2

    loads = [
        pltpu.make_async_copy(src, dst, in_sem.at[i])
        for i, (src, dst) in enumerate(
            [(gate_hbm, gate_ref), (hid_hbm, hid_ref), (k_hbm, k_ref), (v_hbm, v_ref),
             (q_hbm, q_ref), (g_hbm, g_ref), (slot_hbm, slot_ref)]
        )
    ]
    for c in loads:
        c.start()

    me = lax.axis_index("seq")
    hd = lax.axis_index("head")
    odd = me % 2
    z = me // 2
    pair = me + 1 - 2 * odd
    above = jnp.minimum(z + 1, zn - 1) * 2 + odd
    below = jnp.maximum(z - 1, 0) * 2 + odd
    is_top = z == zn - 1
    not_top = z < zn - 1
    not_low = z > 0
    low_half = z < zn // 2
    high_half = z >= zn // 2
    bit = [(z // (1 << j)) % 2 for j in range(nb)]
    jstar = jnp.int32(nb)
    for j in reversed(range(nb)):
        jstar = jnp.where(bit[j] == 0, j, jstar)
    peers = [lax.rem(hd + d, head_n) for d in range(1, head_n)]

    barrier = pltpu.get_barrier_semaphore()
    pl.semaphore_signal(barrier, inc=1, device_id={"seq": pair}, device_id_type=MESH)
    for p in peers:
        pl.semaphore_signal(barrier, inc=1, device_id={"head": p}, device_id_type=MESH)

    @pl.when(not_top)
    def _():
        pl.semaphore_signal(barrier, inc=1, device_id={"seq": above}, device_id_type=MESH)

    @pl.when(not_low)
    def _():
        pl.semaphore_signal(barrier, inc=1, device_id={"seq": below}, device_id_type=MESH)

    def cs(k):
        return pl.ds(k * ch, ch)

    def group(k):
        return range(k * ch, (k + 1) * ch)

    def copy(src, dst, ss, rs, where):
        return pltpu.make_async_remote_copy(
            src_ref=src, dst_ref=dst, send_sem=ss, recv_sem=rs, device_id=where, device_id_type=MESH
        )

    def lp_copy(d):
        return copy(
            lp_send.at[peers[d - 1]], lp_recv.at[d - 1], lp_ss.at[d - 1], lp_rs.at[d - 1],
            {"head": peers[d - 1]},
        )

    def lg_copy(d):
        return copy(
            lg_all.at[hd], lg_all.at[hd], lg_ss.at[d - 1], lg_rs.at[d - 1], {"head": peers[d - 1]}
        )

    def lg_wait(d):
        src = lax.rem(hd + head_n - d, head_n)
        copy(lg_all.at[src], lg_all.at[src], lg_ss.at[d - 1], lg_rs.at[d - 1], {"head": peers[d - 1]}).wait_recv()

    def pair_copy(k):
        return copy(s_bf.at[cs(k)], pair_recv.at[cs(k)], pr_ss.at[k], pr_rs.at[k], {"seq": pair})

    def up_copy(j, k):
        return copy(ls.at[j, cs(k)], ls.at[j, cs(k)], up_ss.at[j, k], up_rs.at[j, k], {"seq": above})

    def h_copy(k):
        j = jnp.minimum(jstar, nb - 1)
        return copy(h_send.at[cs(k)], ls.at[j, cs(k)], up_ss.at[j, k], up_rs.at[j, k], {"seq": above})

    def down_copy(j, k):
        return copy(r_send.at[j, cs(k)], r_recv.at[j, cs(k)], dn_ss.at[j, k], dn_rs.at[j, k], {"seq": below})

    def m_copy(k):
        return copy(m_send.at[cs(k)], m_recv.at[cs(k)], m_ss.at[k], m_rs.at[k], {"seq": pair})

    def out_copy(i, src, dst, k):
        sl = pl.ds(k * ch * DK, ch * DK)
        return pltpu.make_async_copy(src.at[:, sl], dst.at[:, sl], out_sem.at[i, k])

    def hs(ref, h):
        return ref[:, h * DK:(h + 1) * DK]

    wide = head_n * rows
    r_from = lax.broadcasted_iota(jnp.int32, (wide, wide), 0)
    r_to = lax.broadcasted_iota(jnp.int32, (1, wide), 1)
    in_dev = r_to % rows
    loads[6].wait()
    lev_of = in_dev // heads
    slot_of = jnp.zeros((1, wide), jnp.int32)
    for l in range(levels):
        slot_of = jnp.where(lev_of == l, slot_ref[l], slot_of)
    target = (r_to // rows) * rows + (in_dev % heads) * levels + slot_of
    perm = jnp.where(r_from == target, 1.0, 0.0).astype(BF16)
    loads[0].wait()
    loads[1].wait()
    gatep[...] = dot(gate_ref[...], perm, 1, 0).astype(BF16)
    partial = dot(hid_ref[...], gatep[...], 1, 0).T
    for p in range(head_n):
        lp_send[p] = partial[p * rows:(p + 1) * rows, :]

    loads[2].wait()
    loads[3].wait()

    def states(hh):
        for h in hh:
            s = dot(hs(k_ref, h), hs(v_ref, h), 0, 0)
            s_f32[h] = s
            s_bf[h] = s.astype(BF16)

    states(group(0))

    pl.semaphore_wait(
        barrier, head_n + jnp.where(not_top, 1, 0) + jnp.where(not_low, 1, 0)
    )
    for d in range(1, head_n):
        lp_copy(d).start()

    sends_s = jnp.logical_or(odd == 0, not_top)
    gets_s = jnp.logical_or(odd == 1, not_top)
    sends_m = jnp.logical_or(odd == 1, not_top)
    gets_m = jnp.logical_or(odd == 0, not_top)

    def send_pair(k):
        @pl.when(sends_s)
        def _():
            pair_copy(k).start()

    send_pair(0)
    states(range(ch, heads))
    for k in range(1, chunks):
        send_pair(k)

    for j in range(nb):
        @pl.when(bit[j] == 0)
        def _(j=j):
            ls[j] = jnp.zeros(ls.shape[1:], BF16)

    r_recv[nb] = jnp.zeros(r_recv.shape[1:], BF16)

    @pl.when(jnp.logical_and(is_top, odd == 0))
    def _():
        pair_recv[...] = jnp.zeros(pair_recv.shape, BF16)

    @pl.when(jnp.logical_and(is_top, odd == 1))
    def _():
        m_recv[...] = jnp.zeros(m_recv.shape, BF16)

    t_pos = lax.broadcasted_iota(jnp.int32, (tok, tok), 0)
    s_pos = lax.broadcasted_iota(jnp.int32, (tok, tok), 1)
    causal = jnp.where(t_pos >= s_pos, 1.0 / tok, 0.0)
    causal_t = jnp.where(s_pos >= t_pos, 1.0 / tok, 0.0)

    def inside(hh):
        sc = [dot(hs(q_ref, h), hs(k_ref, h), 1, 1) for h in hh]
        st = [dot(hs(k_ref, h), hs(q_ref, h), 1, 1) for h in hh]
        at = [(s * causal).astype(BF16) for s in sc]
        for h, s in zip(hh, st):
            att_t[h] = (s * causal_t).astype(BF16)
        for h, a in zip(hh, at):
            intra[h] = dot(a, hs(v_ref, h), 1, 0)

    def f1(k):
        @pl.when(gets_s)
        def _():
            pair_copy(k).wait_recv()

        @pl.when(jnp.logical_and(not_top, jstar == 0))
        def _():
            h_send[cs(k)] = (s_f32[cs(k)] + pair_recv[cs(k)].astype(F32)).astype(BF16)
            h_copy(k).start()

    def f2(k):
        @pl.when(not_top)
        def _():
            for j in range(nb):
                @pl.when(bit[j] == 1)
                def _(j=j):
                    up_copy(j, k).wait_recv()

            for j in range(nb):
                @pl.when(jnp.logical_and(bit[j] == 1, j > jstar))
                def _(j=j):
                    up_copy(j, k).start()

            @pl.when(jstar > 0)
            def _():
                total = s_f32[cs(k)] + pair_recv[cs(k)].astype(F32)
                for j in range(nb):
                    total = total + jnp.where(j < jstar, ls[j, cs(k)].astype(F32), 0.0)
                h_send[cs(k)] = total.astype(BF16)
                h_copy(k).start()

    loads[4].wait()
    half = max(heads // 2, 1)
    inside(range(half))
    f1(0)
    inside(range(half, heads))
    loads[5].wait()

    mine = lp_send[hd]
    for d in range(1, head_n):
        lp_copy(d).wait_recv()
    for d in range(1, head_n):
        mine = mine + lp_recv[d - 1]
    soft = jnp.maximum(mine, 0.0) + jnp.log1p(jnp.exp(-jnp.abs(mine)))
    pad = jnp.zeros((DK - rows, tok), F32)
    soft_t = jnp.concatenate([soft, pad], 0).T if rows < DK else soft.T
    sig = jax.nn.sigmoid(mine)

    def weigh(k):
        for h in group(k):
            gh = hs(g_ref, h).astype(F32)
            for l in range(levels):
                c = l * heads + h
                w = jnp.broadcast_to(soft_t[:, c:c + 1], (tok, DK))
                w_all[l, h] = w
                if l == 0:
                    w0g[h] = (w * gh).astype(BF16)
                else:
                    wlg[h, :, (l - 1) * DK:l * DK] = (w * gh).astype(BF16)

    def level_grads(k):
        weigh(k)
        for h in group(k):
            grads = dot(hs(q_ref, h), wlg[h], 0, 0)
            lev1[h] = grads[:, :DK] * (1.0 / tok)
            for j in range(nb):
                lev[j, h] = grads[:, (j + 1) * DK:(j + 2) * DK] * (1.0 / (tok * 2 << j))

        @pl.when(is_top)
        def _():
            for j in reversed(range(nb)):
                r_send[j, cs(k)] = lev[j, cs(k)].astype(BF16)
                @pl.when(not_low)
                def _(j=j):
                    down_copy(j, k).start()

    def back(k):
        @pl.when(not_top)
        def _():
            for j in reversed(range(nb)):
                @pl.when(((z + 1) // (1 << j)) % 2 == 1)
                def _(j=j):
                    down_copy(j, k).wait_recv()

                @pl.when(bit[j] == 1)
                def _(j=j):
                    came = jnp.where(j < jstar, jstar, j)
                    r_send[j, cs(k)] = (lev[j, cs(k)] + r_recv[came, cs(k)].astype(F32)).astype(BF16)
                    down_copy(j, k).start()

        @pl.when(sends_m)
        def _():
            got = r_recv[jstar, cs(k)].astype(F32)
            own = jnp.where(odd == 1, 1.0, 0.0)
            m_send[cs(k)] = (got + own * lev1[cs(k)]).astype(BF16)
            m_copy(k).start()

    def span_grads(k):
        sc = [dot(w0g[h], hs(v_ref, h), 1, 1) for h in group(k)]
        st = [dot(hs(v_ref, h), w0g[h], 1, 1) for h in group(k)]
        for h, s, t in zip(group(k), sc, st):
            score[h] = (s * causal).astype(BF16)
            score_t[h] = (t * causal_t).astype(BF16)

    def low(f, k):
        @pl.when(low_half)
        def _():
            f(k)

    def high(f, k):
        @pl.when(high_half)
        def _():
            f(k)

    for k in range(chunks):
        level_grads(k)
        if k + 1 < chunks:
            f1(k + 1)
        if k >= 1:
            low(f2, k - 1)
    low(f2, chunks - 1)
    for k in range(chunks):
        high(back, k)
        if k < chunks // 2:
            span_grads(k)
    for k in range(chunks):
        low(back, k)
        high(f2, k)
        if k >= chunks // 2:
            span_grads(k)

    col = lax.broadcasted_iota(jnp.int32, (tok, DK), 1)
    scales = [jnp.where(odd == 1, 1.0 / tok, 0.0)] + [1.0 / (tok * 2 << j) for j in range(nb)]
    wg = jnp.zeros((tok, DK), F32)
    for k in range(chunks):
        @pl.when(is_top)
        def _(k=k):
            for j in range(nb):
                up_copy(j, k).wait_recv()

        cats = []
        for h in group(k):
            parts = [pair_recv[h]] + [ls[j, h] for j in range(nb)]
            cats.append(jnp.concatenate(
                [(p.astype(F32) * s).astype(BF16) for p, s in zip(parts, scales)], 1))
        los = [dot(hs(q_ref, h), c, 1, 0) for h, c in zip(group(k), cats)]
        gqs = [dot(score[h], hs(k_ref, h), 1, 0) + dot(wlg[h], c, 1, 1) for h, c in zip(group(k), cats)]
        for h, lo, gq in zip(group(k), los, gqs):
            sl = slice(h * DK, (h + 1) * DK)
            gh = hs(g_ref, h).astype(F32)
            part = intra[h]
            out = w_all[0, h] * part
            wg = jnp.where(col == h, jnp.sum(gh * part, 1, keepdims=True), wg)
            for l in range(1, levels):
                lol = lo[:, (l - 1) * DK:l * DK]
                out = out + w_all[l, h] * lol
                wg = jnp.where(col == l * heads + h, jnp.sum(gh * lol, 1, keepdims=True), wg)
            mixed_ref[:, sl] = out.astype(BF16)
            gq_ref[:, sl] = gq.astype(BF16)
        out_copy(0, mixed_ref, mixed_hbm, k).start()
        out_copy(1, gq_ref, gq_hbm, k).start()

    lg_all[hd] = (wg.T[:rows, :] * sig).astype(BF16)
    for d in range(1, head_n):
        lg_copy(d).start()

    for k in range(chunks):
        @pl.when(gets_m)
        def _(k=k):
            m_copy(k).wait_recv()

        sgs = [(r_recv[jstar, h].astype(F32) + m_recv[h].astype(F32)).astype(BF16) for h in group(k)]
        gks = [dot(score_t[h], hs(q_ref, h), 1, 0) + dot(hs(v_ref, h), sg, 1, 1) for h, sg in zip(group(k), sgs)]
        gvs = [dot(att_t[h], w0g[h], 1, 0) + dot(hs(k_ref, h), sg, 1, 0) for h, sg in zip(group(k), sgs)]
        for h, gk, gv in zip(group(k), gks, gvs):
            sl = slice(h * DK, (h + 1) * DK)
            gk_ref[:, sl] = gk.astype(BF16)
            gv_ref[:, sl] = gv.astype(BF16)
        out_copy(2, gk_ref, gk_hbm, k).start()
        out_copy(3, gv_ref, gv_hbm, k).start()

    for d in range(1, head_n):
        lg_wait(d)
    every = jnp.concatenate([lg_all[p] for p in range(head_n)], 0)
    ghid_ref[...] = dot(every, gatep[...], 0, 1).astype(BF16)
    last = pltpu.make_async_copy(ghid_ref, ghid_hbm, hid_sem)
    last.start()

    for d in range(1, head_n):
        lp_copy(d).wait_send()
        lg_copy(d).wait_send()
    for k in range(chunks):
        @pl.when(sends_s)
        def _(k=k):
            pair_copy(k).wait_send()

        @pl.when(sends_m)
        def _(k=k):
            m_copy(k).wait_send()

        for j in range(nb):
            @pl.when(jnp.logical_and(not_top, ((z + 1) // (1 << j)) % 2 == 1))
            def _(j=j, k=k):
                up_copy(j, k).wait_send()

            @pl.when(jnp.logical_and(not_low, bit[j] == 1))
            def _(j=j, k=k):
                down_copy(j, k).wait_send()
        for i, (src, dst) in enumerate(
            [(mixed_ref, mixed_hbm), (gq_ref, gq_hbm), (gk_ref, gk_hbm), (gv_ref, gv_hbm)]
        ):
            out_copy(i, src, dst, k).wait()
    last.wait()


def hand_over(*refs):
    n = len(refs) // 2
    sem = refs[-1]
    copies = [pltpu.make_async_copy(refs[i], refs[n + i], sem.at[i]) for i in range(n)]
    for c in copies:
        c.start()
    for c in copies:
        c.wait()


def local(seq_n, head_n, queries, keys, values, hidden, gate_weight, level_slot, out_grad):
    tok, width = queries.shape
    heads = width // DK
    levels = level_slot.shape[0]
    nb = levels - 2
    rows = heads * levels
    chunks = heads // min(CHUNK_HEADS, heads)
    feats = hidden.shape[1]
    wide = head_n * rows
    hbm = pl.BlockSpec(memory_space=pl.ANY)
    blk = (heads, DK, DK)
    sem = pltpu.SemaphoreType.DMA
    outs = [jax.ShapeDtypeStruct((tok, width), BF16)] * 4 + [
        jax.ShapeDtypeStruct((tok, feats), BF16)
    ]
    made = pl.pallas_call(
        functools.partial(mix_kernel, seq_n, head_n),
        out_shape=outs,
        in_specs=[pl.BlockSpec(memory_space=pltpu.HBM)] * 7,
        out_specs=[hbm] * 5,
        scratch_shapes=[
            pltpu.SMEM((levels,), jnp.int32),
            pltpu.VMEM((tok, width), BF16),
            pltpu.VMEM((tok, width), BF16),
            pltpu.VMEM((tok, width), BF16),
            pltpu.VMEM((tok, feats), BF16),
            pltpu.VMEM((feats, wide), BF16),
            pltpu.VMEM((tok, width), BF16),
            pltpu.VMEM((tok, width), BF16),
            pltpu.VMEM((tok, width), BF16),
            pltpu.VMEM((tok, width), BF16),
            pltpu.VMEM((tok, width), BF16),
            pltpu.VMEM((tok, feats), BF16),
            pltpu.VMEM((feats, wide), BF16),
            pltpu.VMEM((head_n, rows, tok), F32),
            pltpu.VMEM((head_n - 1, rows, tok), F32),
            pltpu.VMEM((head_n, rows, tok), BF16),
            pltpu.VMEM(blk, F32),
            pltpu.VMEM(blk, BF16),
            pltpu.VMEM(blk, BF16),
            pltpu.VMEM((nb,) + blk, BF16),
            pltpu.VMEM(blk, BF16),
            pltpu.VMEM((nb,) + blk, BF16),
            pltpu.VMEM((nb + 1,) + blk, BF16),
            pltpu.VMEM(blk, BF16),
            pltpu.VMEM(blk, BF16),
            pltpu.VMEM(blk, F32),
            pltpu.VMEM((nb,) + blk, F32),
            pltpu.VMEM(blk, F32),
            pltpu.VMEM(blk, BF16),
            pltpu.VMEM(blk, BF16),
            pltpu.VMEM(blk, BF16),
            pltpu.VMEM((levels,) + blk, F32),
            pltpu.VMEM(blk, BF16),
            pltpu.VMEM((heads, tok, (levels - 1) * DK), BF16),
            sem((7,)), sem((4, chunks)), sem(()),
            sem((head_n - 1,)), sem((head_n - 1,)),
            sem((head_n - 1,)), sem((head_n - 1,)),
            sem((chunks,)), sem((chunks,)),
            sem((nb, chunks)), sem((nb, chunks)),
            sem((nb, chunks)), sem((nb, chunks)),
            sem((chunks,)), sem((chunks,)),
        ],
        compiler_params=pltpu.CompilerParams(
            collective_id=0, has_side_effects=True, vmem_limit_bytes=VMEM_ALL
        ),
    )(level_slot, queries, keys, values, hidden, gate_weight, out_grad)
    return pl.pallas_call(
        hand_over,
        out_shape=outs,
        in_specs=[hbm] * 5,
        out_specs=[hbm] * 5,
        scratch_shapes=[sem((5,))],
        compiler_params=pltpu.CompilerParams(vmem_limit_bytes=VMEM_ALL),
    )(*made)


def solution(mesh):
    both = P("seq", "head")
    return jax.shard_map(
        functools.partial(local, mesh.shape["seq"], mesh.shape["head"]),
        mesh=mesh,
        in_specs=(both, both, both, both, P("head", None), P(), both),
        out_specs=(both,) * 5,
        check_vma=False,
    )
```

```python
import functools

import jax
import jax.numpy as jnp
from jax import lax
from jax.experimental import pallas as pl
from jax.experimental.pallas import tpu as pltpu
from jax.sharding import PartitionSpec as P

DK = 128
MESH = pl.DeviceIdType.MESH
F32 = jnp.float32
BF16 = jnp.bfloat16
CHUNK_HEADS = 2
VMEM_ALL = (64 << 20) - (1 << 19)


def dot(a, b, ca, cb):
    return lax.dot_general(a, b, (((ca,), (cb,)), ((), ())), preferred_element_type=F32)


def mix_kernel(
    seq_n, head_n,
    slot_hbm, q_hbm, k_hbm, v_hbm, hid_hbm, gate_hbm, g_hbm,
    mixed_hbm, gq_hbm, gk_hbm, gv_hbm, ghid_hbm,
    slot_ref, q_ref, k_ref, v_ref, hid_ref, gate_ref, g_ref,
    mixed_ref, gq_ref, gk_ref, gv_ref, ghid_ref,
    gatep, lp_send, lp_recv, lg_all,
    s_f32, s_bf, pair_recv, ls, h_send, r_send, r_recv, m_send, m_recv,
    intra, lev, lev1, att_t, score, score_t, w_all, w0g, wlg,
    in_sem, out_sem, hid_sem,
    lp_ss, lp_rs, lg_ss, lg_rs, pr_ss, pr_rs, up_ss, up_rs, dn_ss, dn_rs, m_ss, m_rs,
):
    tok = q_ref.shape[0]
    heads = q_ref.shape[1] // DK
    levels = lev.shape[0] + 2
    nb = levels - 2
    rows = heads * levels
    ch = min(CHUNK_HEADS, heads)
    chunks = heads // ch
    zn = seq_n // 2

    loads = [
        pltpu.make_async_copy(src, dst, in_sem.at[i])
        for i, (src, dst) in enumerate(
            [(gate_hbm, gate_ref), (hid_hbm, hid_ref), (k_hbm, k_ref), (v_hbm, v_ref),
             (q_hbm, q_ref), (g_hbm, g_ref), (slot_hbm, slot_ref)]
        )
    ]
    for c in loads:
        c.start()

    me = lax.axis_index("seq")
    hd = lax.axis_index("head")
    odd = me % 2
    z = me // 2
    pair = me + 1 - 2 * odd
    above = jnp.minimum(z + 1, zn - 1) * 2 + odd
    below = jnp.maximum(z - 1, 0) * 2 + odd
    is_top = z == zn - 1
    not_top = z < zn - 1
    not_low = z > 0
    low_half = z < zn // 2
    high_half = z >= zn // 2
    bit = [(z // (1 << j)) % 2 for j in range(nb)]
    jstar = jnp.int32(nb)
    for j in reversed(range(nb)):
        jstar = jnp.where(bit[j] == 0, j, jstar)
    peers = [lax.rem(hd + d, head_n) for d in range(1, head_n)]

    barrier = pltpu.get_barrier_semaphore()
    pl.semaphore_signal(barrier, inc=1, device_id={"seq": pair}, device_id_type=MESH)
    for p in peers:
        pl.semaphore_signal(barrier, inc=1, device_id={"head": p}, device_id_type=MESH)

    @pl.when(not_top)
    def _():
        pl.semaphore_signal(barrier, inc=1, device_id={"seq": above}, device_id_type=MESH)

    @pl.when(not_low)
    def _():
        pl.semaphore_signal(barrier, inc=1, device_id={"seq": below}, device_id_type=MESH)

    def cs(k):
        return pl.ds(k * ch, ch)

    def group(k):
        return range(k * ch, (k + 1) * ch)

    def copy(src, dst, ss, rs, where):
        return pltpu.make_async_remote_copy(
            src_ref=src, dst_ref=dst, send_sem=ss, recv_sem=rs, device_id=where, device_id_type=MESH
        )

    def lp_copy(d):
        return copy(
            lp_send.at[peers[d - 1]], lp_recv.at[d - 1], lp_ss.at[d - 1], lp_rs.at[d - 1],
            {"head": peers[d - 1]},
        )

    def lg_copy(d):
        return copy(
            lg_all.at[hd], lg_all.at[hd], lg_ss.at[d - 1], lg_rs.at[d - 1], {"head": peers[d - 1]}
        )

    def lg_wait(d):
        src = lax.rem(hd + head_n - d, head_n)
        copy(lg_all.at[src], lg_all.at[src], lg_ss.at[d - 1], lg_rs.at[d - 1], {"head": peers[d - 1]}).wait_recv()

    def pair_copy(k):
        return copy(s_bf.at[cs(k)], pair_recv.at[cs(k)], pr_ss.at[k], pr_rs.at[k], {"seq": pair})

    def up_copy(j, k):
        return copy(ls.at[j, cs(k)], ls.at[j, cs(k)], up_ss.at[j, k], up_rs.at[j, k], {"seq": above})

    def h_copy(k):
        j = jnp.minimum(jstar, nb - 1)
        return copy(h_send.at[cs(k)], ls.at[j, cs(k)], up_ss.at[j, k], up_rs.at[j, k], {"seq": above})

    def down_copy(j, k):
        return copy(r_send.at[j, cs(k)], r_recv.at[j, cs(k)], dn_ss.at[j, k], dn_rs.at[j, k], {"seq": below})

    def m_copy(k):
        return copy(m_send.at[cs(k)], m_recv.at[cs(k)], m_ss.at[k], m_rs.at[k], {"seq": pair})

    def out_copy(i, src, dst, k):
        sl = pl.ds(k * ch * DK, ch * DK)
        return pltpu.make_async_copy(src.at[:, sl], dst.at[:, sl], out_sem.at[i, k])

    def hs(ref, h):
        return ref[:, h * DK:(h + 1) * DK]

    wide = head_n * rows
    r_from = lax.broadcasted_iota(jnp.int32, (wide, wide), 0)
    r_to = lax.broadcasted_iota(jnp.int32, (1, wide), 1)
    in_dev = r_to % rows
    loads[6].wait()
    lev_of = in_dev // heads
    slot_of = jnp.zeros((1, wide), jnp.int32)
    for l in range(levels):
        slot_of = jnp.where(lev_of == l, slot_ref[l], slot_of)
    target = (r_to // rows) * rows + (in_dev % heads) * levels + slot_of
    perm = jnp.where(r_from == target, 1.0, 0.0).astype(BF16)
    loads[0].wait()
    loads[1].wait()
    gatep[...] = dot(gate_ref[...], perm, 1, 0).astype(BF16)
    partial = dot(hid_ref[...], gatep[...], 1, 0).T
    for p in range(head_n):
        lp_send[p] = partial[p * rows:(p + 1) * rows, :]

    loads[2].wait()
    loads[3].wait()

    def states(hh):
        for h in hh:
            s = dot(hs(k_ref, h), hs(v_ref, h), 0, 0)
            s_f32[h] = s
            s_bf[h] = s.astype(BF16)

    states(group(0))

    pl.semaphore_wait(
        barrier, head_n + jnp.where(not_top, 1, 0) + jnp.where(not_low, 1, 0)
    )
    for d in range(1, head_n):
        lp_copy(d).start()

    sends_s = jnp.logical_or(odd == 0, not_top)
    gets_s = jnp.logical_or(odd == 1, not_top)
    sends_m = jnp.logical_or(odd == 1, not_top)
    gets_m = jnp.logical_or(odd == 0, not_top)

    def send_pair(k):
        @pl.when(sends_s)
        def _():
            pair_copy(k).start()

    send_pair(0)
    states(range(ch, heads))
    for k in range(1, chunks):
        send_pair(k)

    for j in range(nb):
        @pl.when(bit[j] == 0)
        def _(j=j):
            ls[j] = jnp.zeros(ls.shape[1:], BF16)

    r_recv[nb] = jnp.zeros(r_recv.shape[1:], BF16)

    @pl.when(jnp.logical_and(is_top, odd == 0))
    def _():
        pair_recv[...] = jnp.zeros(pair_recv.shape, BF16)

    @pl.when(jnp.logical_and(is_top, odd == 1))
    def _():
        m_recv[...] = jnp.zeros(m_recv.shape, BF16)

    t_pos = lax.broadcasted_iota(jnp.int32, (tok, tok), 0)
    s_pos = lax.broadcasted_iota(jnp.int32, (tok, tok), 1)
    causal = jnp.where(t_pos >= s_pos, 1.0 / tok, 0.0)
    causal_t = jnp.where(s_pos >= t_pos, 1.0 / tok, 0.0)

    def inside(hh):
        sc = [dot(hs(q_ref, h), hs(k_ref, h), 1, 1) for h in hh]
        st = [dot(hs(k_ref, h), hs(q_ref, h), 1, 1) for h in hh]
        at = [(s * causal).astype(BF16) for s in sc]
        for h, s in zip(hh, st):
            att_t[h] = (s * causal_t).astype(BF16)
        for h, a in zip(hh, at):
            intra[h] = dot(a, hs(v_ref, h), 1, 0)

    def f1(k):
        @pl.when(gets_s)
        def _():
            pair_copy(k).wait_recv()

        @pl.when(jnp.logical_and(not_top, jstar == 0))
        def _():
            h_send[cs(k)] = (s_f32[cs(k)] + pair_recv[cs(k)].astype(F32)).astype(BF16)
            h_copy(k).start()

    def f2(k):
        @pl.when(not_top)
        def _():
            for j in range(nb):
                @pl.when(bit[j] == 1)
                def _(j=j):
                    up_copy(j, k).wait_recv()

            for j in range(nb):
                @pl.when(jnp.logical_and(bit[j] == 1, j > jstar))
                def _(j=j):
                    up_copy(j, k).start()

            @pl.when(jstar > 0)
            def _():
                total = s_f32[cs(k)] + pair_recv[cs(k)].astype(F32)
                for j in range(nb):
                    total = total + jnp.where(j < jstar, ls[j, cs(k)].astype(F32), 0.0)
                h_send[cs(k)] = total.astype(BF16)
                h_copy(k).start()

    loads[4].wait()
    half = max(heads // 2, 1)
    inside(range(half))
    loads[5].wait()

    mine = lp_send[hd]
    for d in range(1, head_n):
        lp_copy(d).wait_recv()
    for d in range(1, head_n):
        mine = mine + lp_recv[d - 1]
    soft = jnp.maximum(mine, 0.0) + jnp.log1p(jnp.exp(-jnp.abs(mine)))
    pad = jnp.zeros((DK - rows, tok), F32)
    soft_t = jnp.concatenate([soft, pad], 0).T if rows < DK else soft.T
    sig = jax.nn.sigmoid(mine)

    def weigh(k):
        for h in group(k):
            gh = hs(g_ref, h).astype(F32)
            for l in range(levels):
                c = l * heads + h
                w = jnp.broadcast_to(soft_t[:, c:c + 1], (tok, DK))
                w_all[l, h] = w
                if l == 0:
                    w0g[h] = (w * gh).astype(BF16)
                else:
                    wlg[h, :, (l - 1) * DK:l * DK] = (w * gh).astype(BF16)

    def level_grads(k):
        weigh(k)
        for h in group(k):
            grads = dot(hs(q_ref, h), wlg[h], 0, 0)
            lev1[h] = grads[:, :DK] * (1.0 / tok)
            for j in range(nb):
                lev[j, h] = grads[:, (j + 1) * DK:(j + 2) * DK] * (1.0 / (tok * 2 << j))

        @pl.when(is_top)
        def _():
            for j in reversed(range(nb)):
                r_send[j, cs(k)] = lev[j, cs(k)].astype(BF16)
            top_send(nb - 1, k)

    def top_send(j, k):
        @pl.when(not_low)
        def _():
            down_copy(j, k).start()

    def relay(k):
        @pl.when(not_top)
        def _():
            for j in reversed(range(nb)):
                needed = ((z + 1) // (1 << j)) % 2 == 1
                if j == 0:
                    needed = jnp.logical_and(needed, jstar > 0)
                @pl.when(needed)
                def _(j=j):
                    down_copy(j, k).wait_recv()

                @pl.when(bit[j] == 1)
                def _(j=j):
                    came = jnp.where(j < jstar, jstar, j)
                    r_send[j, cs(k)] = (lev[j, cs(k)] + r_recv[came, cs(k)].astype(F32)).astype(BF16)
                    down_copy(j, k).start()

    def meet(k):
        @pl.when(jstar == 0)
        def _():
            down_copy(0, k).wait_recv()

        @pl.when(sends_m)
        def _():
            got = r_recv[jstar, cs(k)].astype(F32)
            own = jnp.where(odd == 1, 1.0, 0.0)
            m_send[cs(k)] = (got + own * lev1[cs(k)]).astype(BF16)
            m_copy(k).start()

    def span_grads(k):
        sc = [dot(w0g[h], hs(v_ref, h), 1, 1) for h in group(k)]
        st = [dot(hs(v_ref, h), w0g[h], 1, 1) for h in group(k)]
        for h, s, t in zip(group(k), sc, st):
            score[h] = (s * causal).astype(BF16)
            score_t[h] = (t * causal_t).astype(BF16)

    def low(f, k):
        @pl.when(low_half)
        def _():
            f(k)

    def high(f, k):
        @pl.when(high_half)
        def _():
            f(k)

    for k in range(chunks):
        level_grads(k)
        f1(k)
        if k >= 1:
            low(f2, k - 1)
    low(f2, chunks - 1)

    @pl.when(is_top)
    def _():
        for j in reversed(range(nb - 1)):
            for k in range(chunks):
                top_send(j, k)

    rest = list(range(half, heads))
    for k in range(chunks):
        relay(k)
        high(f2, k)
        span_grads(k)
        part, rest = rest[:ch], rest[ch:]
        if part:
            inside(part)

    col = lax.broadcasted_iota(jnp.int32, (tok, DK), 1)
    scales = [jnp.where(odd == 1, 1.0 / tok, 0.0)] + [1.0 / (tok * 2 << j) for j in range(nb)]
    wg = jnp.zeros((tok, DK), F32)
    for k in range(chunks):
        @pl.when(is_top)
        def _(k=k):
            for j in range(nb):
                up_copy(j, k).wait_recv()

        cats = []
        for h in group(k):
            parts = [pair_recv[h]] + [ls[j, h] for j in range(nb)]
            cats.append(jnp.concatenate(
                [(p.astype(F32) * s).astype(BF16) for p, s in zip(parts, scales)], 1))
        los = [dot(hs(q_ref, h), c, 1, 0) for h, c in zip(group(k), cats)]
        gqs = [dot(score[h], hs(k_ref, h), 1, 0) + dot(wlg[h], c, 1, 1) for h, c in zip(group(k), cats)]
        for h, lo, gq in zip(group(k), los, gqs):
            sl = slice(h * DK, (h + 1) * DK)
            gh = hs(g_ref, h).astype(F32)
            part = intra[h]
            out = w_all[0, h] * part
            wg = jnp.where(col == h, jnp.sum(gh * part, 1, keepdims=True), wg)
            for l in range(1, levels):
                lol = lo[:, (l - 1) * DK:l * DK]
                out = out + w_all[l, h] * lol
                wg = jnp.where(col == l * heads + h, jnp.sum(gh * lol, 1, keepdims=True), wg)
            mixed_ref[:, sl] = out.astype(BF16)
            gq_ref[:, sl] = gq.astype(BF16)
        out_copy(0, mixed_ref, mixed_hbm, k).start()
        out_copy(1, gq_ref, gq_hbm, k).start()
        meet(k)

    lg_all[hd] = (wg.T[:rows, :] * sig).astype(BF16)
    for d in range(1, head_n):
        lg_copy(d).start()

    for k in range(chunks):
        @pl.when(gets_m)
        def _(k=k):
            m_copy(k).wait_recv()

        sgs = [(r_recv[jstar, h].astype(F32) + m_recv[h].astype(F32)).astype(BF16) for h in group(k)]
        gks = [dot(score_t[h], hs(q_ref, h), 1, 0) + dot(hs(v_ref, h), sg, 1, 1) for h, sg in zip(group(k), sgs)]
        gvs = [dot(att_t[h], w0g[h], 1, 0) + dot(hs(k_ref, h), sg, 1, 0) for h, sg in zip(group(k), sgs)]
        for h, gk, gv in zip(group(k), gks, gvs):
            sl = slice(h * DK, (h + 1) * DK)
            gk_ref[:, sl] = gk.astype(BF16)
            gv_ref[:, sl] = gv.astype(BF16)
        out_copy(2, gk_ref, gk_hbm, k).start()
        out_copy(3, gv_ref, gv_hbm, k).start()
        if k == max(chunks // 2 - 1, 0):
            for d in range(1, head_n):
                lg_wait(d)
            every = jnp.concatenate([lg_all[p] for p in range(head_n)], 0)
            ghid_ref[...] = dot(every, gatep[...], 0, 1).astype(BF16)
            last = pltpu.make_async_copy(ghid_ref, ghid_hbm, hid_sem)
            last.start()

    for d in range(1, head_n):
        lp_copy(d).wait_send()
        lg_copy(d).wait_send()
    for k in range(chunks):
        @pl.when(sends_s)
        def _(k=k):
            pair_copy(k).wait_send()

        @pl.when(sends_m)
        def _(k=k):
            m_copy(k).wait_send()

        for j in range(nb):
            @pl.when(jnp.logical_and(not_top, ((z + 1) // (1 << j)) % 2 == 1))
            def _(j=j, k=k):
                up_copy(j, k).wait_send()

            @pl.when(jnp.logical_and(not_low, bit[j] == 1))
            def _(j=j, k=k):
                down_copy(j, k).wait_send()
        for i, (src, dst) in enumerate(
            [(mixed_ref, mixed_hbm), (gq_ref, gq_hbm), (gk_ref, gk_hbm), (gv_ref, gv_hbm)]
        ):
            out_copy(i, src, dst, k).wait()
    last.wait()


def hand_over(*refs):
    n = len(refs) // 3
    sem = refs[-1]
    ins = [pltpu.make_async_copy(refs[i], refs[2 * n + i], sem.at[0, i]) for i in range(n)]
    outs = [pltpu.make_async_copy(refs[2 * n + i], refs[n + i], sem.at[1, i]) for i in range(n)]
    for c in ins:
        c.start()
    for a, b in zip(ins, outs):
        a.wait()
        b.start()
    for c in outs:
        c.wait()


def local(seq_n, head_n, queries, keys, values, hidden, gate_weight, level_slot, out_grad):
    tok, width = queries.shape
    heads = width // DK
    levels = level_slot.shape[0]
    nb = levels - 2
    rows = heads * levels
    chunks = heads // min(CHUNK_HEADS, heads)
    feats = hidden.shape[1]
    wide = head_n * rows
    hbm = pl.BlockSpec(memory_space=pl.ANY)
    blk = (heads, DK, DK)
    sem = pltpu.SemaphoreType.DMA
    outs = [jax.ShapeDtypeStruct((tok, width), BF16)] * 4 + [
        jax.ShapeDtypeStruct((tok, feats), BF16)
    ]
    made = pl.pallas_call(
        functools.partial(mix_kernel, seq_n, head_n),
        out_shape=outs,
        in_specs=[pl.BlockSpec(memory_space=pltpu.HBM)] * 7,
        out_specs=[hbm] * 5,
        scratch_shapes=[
            pltpu.SMEM((levels,), jnp.int32),
            pltpu.VMEM((tok, width), BF16),
            pltpu.VMEM((tok, width), BF16),
            pltpu.VMEM((tok, width), BF16),
            pltpu.VMEM((tok, feats), BF16),
            pltpu.VMEM((feats, wide), BF16),
            pltpu.VMEM((tok, width), BF16),
            pltpu.VMEM((tok, width), BF16),
            pltpu.VMEM((tok, width), BF16),
            pltpu.VMEM((tok, width), BF16),
            pltpu.VMEM((tok, width), BF16),
            pltpu.VMEM((tok, feats), BF16),
            pltpu.VMEM((feats, wide), BF16),
            pltpu.VMEM((head_n, rows, tok), F32),
            pltpu.VMEM((head_n - 1, rows, tok), F32),
            pltpu.VMEM((head_n, rows, tok), BF16),
            pltpu.VMEM(blk, F32),
            pltpu.VMEM(blk, BF16),
            pltpu.VMEM(blk, BF16),
            pltpu.VMEM((nb,) + blk, BF16),
            pltpu.VMEM(blk, BF16),
            pltpu.VMEM((nb,) + blk, BF16),
            pltpu.VMEM((nb + 1,) + blk, BF16),
            pltpu.VMEM(blk, BF16),
            pltpu.VMEM(blk, BF16),
            pltpu.VMEM(blk, F32),
            pltpu.VMEM((nb,) + blk, F32),
            pltpu.VMEM(blk, F32),
            pltpu.VMEM(blk, BF16),
            pltpu.VMEM(blk, BF16),
            pltpu.VMEM(blk, BF16),
            pltpu.VMEM((levels,) + blk, F32),
            pltpu.VMEM(blk, BF16),
            pltpu.VMEM((heads, tok, (levels - 1) * DK), BF16),
            sem((7,)), sem((4, chunks)), sem(()),
            sem((head_n - 1,)), sem((head_n - 1,)),
            sem((head_n - 1,)), sem((head_n - 1,)),
            sem((chunks,)), sem((chunks,)),
            sem((nb, chunks)), sem((nb, chunks)),
            sem((nb, chunks)), sem((nb, chunks)),
            sem((chunks,)), sem((chunks,)),
        ],
        compiler_params=pltpu.CompilerParams(
            collective_id=0, has_side_effects=True, vmem_limit_bytes=VMEM_ALL
        ),
    )(level_slot, queries, keys, values, hidden, gate_weight, out_grad)
    return pl.pallas_call(
        hand_over,
        out_shape=outs,
        in_specs=[hbm] * 5,
        out_specs=[hbm] * 5,
        scratch_shapes=[pltpu.VMEM(o.shape, o.dtype) for o in outs] + [sem((2, 5))],
        compiler_params=pltpu.CompilerParams(vmem_limit_bytes=VMEM_ALL),
    )(*made)


def solution(mesh):
    both = P("seq", "head")
    return jax.shard_map(
        functools.partial(local, mesh.shape["seq"], mesh.shape["head"]),
        mesh=mesh,
        in_specs=(both, both, both, both, P("head", None), P(), both),
        out_specs=(both,) * 5,
        check_vma=False,
    )
```

```python
import functools

import jax
import jax.numpy as jnp
from jax import lax
from jax.experimental import pallas as pl
from jax.experimental.pallas import tpu as pltpu
from jax.sharding import PartitionSpec as P

DK = 128
MESH = pl.DeviceIdType.MESH
F32 = jnp.float32
BF16 = jnp.bfloat16
CHUNK_HEADS = 2
SENT_HEADS = 1
VMEM_ALL = (64 << 20) - (1 << 21)


def dot(a, b, ca, cb):
    return lax.dot_general(a, b, (((ca,), (cb,)), ((), ())), preferred_element_type=F32)


def mix_kernel(
    seq_n, head_n,
    slot_hbm, q_hbm, k_hbm, v_hbm, hid_hbm, gate_hbm, g_hbm,
    mixed_ref, gq_ref, gk_ref, gv_ref, ghid_ref,
    slot_ref, q_ref, k_ref, v_ref, hid_ref, gate_ref, g_ref,
    gatep, lp_send, lp_recv, lg_all,
    s_f32, s_bf, pair_recv, ls, h_send, r_send, r_recv, m_send, m_recv,
    intra, lev, lev1, att_t, score, score_t, w_all, w0g, wlg,
    in_sem,
    lp_ss, lp_rs, lg_ss, lg_rs, pr_ss, pr_rs, up_ss, up_rs, dn_ss, dn_rs, m_ss, m_rs,
):
    tok = q_ref.shape[0]
    heads = q_ref.shape[1] // DK
    levels = lev.shape[0] + 2
    nb = levels - 2
    rows = heads * levels
    ch = min(CHUNK_HEADS, heads)
    chunks = heads // ch
    sent = min(SENT_HEADS, ch)
    pieces = heads // sent
    zn = seq_n // 2

    loads = [
        pltpu.make_async_copy(src, dst, in_sem.at[i])
        for i, (src, dst) in enumerate(
            [(gate_hbm, gate_ref), (hid_hbm, hid_ref), (k_hbm, k_ref), (v_hbm, v_ref),
             (q_hbm, q_ref), (g_hbm, g_ref), (slot_hbm, slot_ref)]
        )
    ]
    for c in loads:
        c.start()

    me = lax.axis_index("seq")
    hd = lax.axis_index("head")
    odd = me % 2
    z = me // 2
    pair = me + 1 - 2 * odd
    above = jnp.minimum(z + 1, zn - 1) * 2 + odd
    below = jnp.maximum(z - 1, 0) * 2 + odd
    is_top = z == zn - 1
    not_top = z < zn - 1
    not_low = z > 0
    low_half = z < zn // 2
    high_half = z >= zn // 2
    bit = [(z // (1 << j)) % 2 for j in range(nb)]
    jstar = jnp.int32(nb)
    for j in reversed(range(nb)):
        jstar = jnp.where(bit[j] == 0, j, jstar)
    peers = [lax.rem(hd + d, head_n) for d in range(1, head_n)]

    barrier = pltpu.get_barrier_semaphore()
    pl.semaphore_signal(barrier, inc=1, device_id={"seq": pair}, device_id_type=MESH)
    for p in peers:
        pl.semaphore_signal(barrier, inc=1, device_id={"head": p}, device_id_type=MESH)

    @pl.when(not_top)
    def _():
        pl.semaphore_signal(barrier, inc=1, device_id={"seq": above}, device_id_type=MESH)

    @pl.when(not_low)
    def _():
        pl.semaphore_signal(barrier, inc=1, device_id={"seq": below}, device_id_type=MESH)

    def cs(k):
        return pl.ds(k * sent, sent)

    def parts_of(k):
        return range(k * ch // sent, (k + 1) * ch // sent)

    def group(k):
        return range(k * ch, (k + 1) * ch)

    def copy(src, dst, ss, rs, where):
        return pltpu.make_async_remote_copy(
            src_ref=src, dst_ref=dst, send_sem=ss, recv_sem=rs, device_id=where, device_id_type=MESH
        )

    def lp_copy(d):
        return copy(
            lp_send.at[peers[d - 1]], lp_recv.at[d - 1], lp_ss.at[d - 1], lp_rs.at[d - 1],
            {"head": peers[d - 1]},
        )

    def lg_copy(d):
        return copy(
            lg_all.at[hd], lg_all.at[hd], lg_ss.at[d - 1], lg_rs.at[d - 1], {"head": peers[d - 1]}
        )

    def lg_wait(d):
        src = lax.rem(hd + head_n - d, head_n)
        copy(lg_all.at[src], lg_all.at[src], lg_ss.at[d - 1], lg_rs.at[d - 1], {"head": peers[d - 1]}).wait_recv()

    def pair_copy(k):
        return copy(s_bf.at[cs(k)], pair_recv.at[cs(k)], pr_ss.at[k], pr_rs.at[k], {"seq": pair})

    def up_copy(j, k):
        return copy(ls.at[j, cs(k)], ls.at[j, cs(k)], up_ss.at[j, k], up_rs.at[j, k], {"seq": above})

    def h_copy(k):
        j = jnp.minimum(jstar, nb - 1)
        return copy(h_send.at[cs(k)], ls.at[j, cs(k)], up_ss.at[j, k], up_rs.at[j, k], {"seq": above})

    def down_copy(j, k):
        return copy(r_send.at[j, cs(k)], r_recv.at[j, cs(k)], dn_ss.at[j, k], dn_rs.at[j, k], {"seq": below})

    def m_copy(k):
        return copy(m_send.at[cs(k)], m_recv.at[cs(k)], m_ss.at[k], m_rs.at[k], {"seq": pair})

    def hs(ref, h):
        return ref[:, h * DK:(h + 1) * DK]

    wide = head_n * rows
    r_from = lax.broadcasted_iota(jnp.int32, (wide, wide), 0)
    r_to = lax.broadcasted_iota(jnp.int32, (1, wide), 1)
    in_dev = r_to % rows
    loads[6].wait()
    lev_of = in_dev // heads
    slot_of = jnp.zeros((1, wide), jnp.int32)
    for l in range(levels):
        slot_of = jnp.where(lev_of == l, slot_ref[l], slot_of)
    target = (r_to // rows) * rows + (in_dev % heads) * levels + slot_of
    perm = jnp.where(r_from == target, 1.0, 0.0).astype(BF16)
    loads[0].wait()
    loads[1].wait()
    gatep[...] = dot(gate_ref[...], perm, 1, 0).astype(BF16)
    partial = dot(hid_ref[...], gatep[...], 1, 0).T
    for p in range(head_n):
        lp_send[p] = partial[p * rows:(p + 1) * rows, :]

    loads[2].wait()
    loads[3].wait()

    def states(hh):
        for h in hh:
            s = dot(hs(k_ref, h), hs(v_ref, h), 0, 0)
            s_f32[h] = s
            s_bf[h] = s.astype(BF16)

    states(group(0))

    pl.semaphore_wait(
        barrier, head_n + jnp.where(not_top, 1, 0) + jnp.where(not_low, 1, 0)
    )
    for d in range(1, head_n):
        lp_copy(d).start()

    sends_s = jnp.logical_or(odd == 0, not_top)
    gets_s = jnp.logical_or(odd == 1, not_top)
    sends_m = jnp.logical_or(odd == 1, not_top)
    gets_m = jnp.logical_or(odd == 0, not_top)

    def send_pair(k):
        @pl.when(sends_s)
        def _():
            pair_copy(k).start()

    for c in parts_of(0):
        send_pair(c)
    states(range(ch, heads))
    for k in range(1, chunks):
        for c in parts_of(k):
            send_pair(c)

    for j in range(nb):
        @pl.when(bit[j] == 0)
        def _(j=j):
            ls[j] = jnp.zeros(ls.shape[1:], BF16)

    r_recv[nb] = jnp.zeros(r_recv.shape[1:], BF16)

    @pl.when(jnp.logical_and(is_top, odd == 0))
    def _():
        pair_recv[...] = jnp.zeros(pair_recv.shape, BF16)

    @pl.when(jnp.logical_and(is_top, odd == 1))
    def _():
        m_recv[...] = jnp.zeros(m_recv.shape, BF16)

    t_pos = lax.broadcasted_iota(jnp.int32, (tok, tok), 0)
    s_pos = lax.broadcasted_iota(jnp.int32, (tok, tok), 1)
    causal = jnp.where(t_pos >= s_pos, 1.0 / tok, 0.0)
    causal_t = jnp.where(s_pos >= t_pos, 1.0 / tok, 0.0)

    def inside(hh):
        sc = [dot(hs(q_ref, h), hs(k_ref, h), 1, 1) for h in hh]
        st = [dot(hs(k_ref, h), hs(q_ref, h), 1, 1) for h in hh]
        at = [(s * causal).astype(BF16) for s in sc]
        for h, s in zip(hh, st):
            att_t[h] = (s * causal_t).astype(BF16)
        for h, a in zip(hh, at):
            intra[h] = dot(a, hs(v_ref, h), 1, 0)

    def f1(k):
        @pl.when(gets_s)
        def _():
            pair_copy(k).wait_recv()

        @pl.when(jnp.logical_and(not_top, jstar == 0))
        def _():
            h_send[cs(k)] = (s_f32[cs(k)] + pair_recv[cs(k)].astype(F32)).astype(BF16)
            h_copy(k).start()

    def f2(k):
        @pl.when(not_top)
        def _():
            for j in range(nb):
                @pl.when(bit[j] == 1)
                def _(j=j):
                    up_copy(j, k).wait_recv()

            for j in range(nb):
                @pl.when(jnp.logical_and(bit[j] == 1, j > jstar))
                def _(j=j):
                    up_copy(j, k).start()

            @pl.when(jstar > 0)
            def _():
                total = s_f32[cs(k)] + pair_recv[cs(k)].astype(F32)
                for j in range(nb):
                    total = total + jnp.where(j < jstar, ls[j, cs(k)].astype(F32), 0.0)
                h_send[cs(k)] = total.astype(BF16)
                h_copy(k).start()

    loads[4].wait()
    half = max(heads // 2, 1)
    inside(range(half))
    loads[5].wait()

    mine = lp_send[hd]
    for d in range(1, head_n):
        lp_copy(d).wait_recv()
    for d in range(1, head_n):
        mine = mine + lp_recv[d - 1]
    soft = jnp.maximum(mine, 0.0) + jnp.log1p(jnp.exp(-jnp.abs(mine)))
    pad = jnp.zeros((DK - rows, tok), F32)
    soft_t = jnp.concatenate([soft, pad], 0).T if rows < DK else soft.T
    sig = jax.nn.sigmoid(mine)

    def weigh(k):
        for h in group(k):
            gh = hs(g_ref, h).astype(F32)
            for l in range(levels):
                c = l * heads + h
                w = jnp.broadcast_to(soft_t[:, c:c + 1], (tok, DK))
                w_all[l, h] = w
                if l == 0:
                    w0g[h] = (w * gh).astype(BF16)
                else:
                    wlg[h, :, (l - 1) * DK:l * DK] = (w * gh).astype(BF16)

    def level_grads(k):
        weigh(k)
        for h in group(k):
            grads = dot(hs(q_ref, h), wlg[h], 0, 0)
            lev1[h] = grads[:, :DK] * (1.0 / tok)
            for j in range(nb):
                lev[j, h] = grads[:, (j + 1) * DK:(j + 2) * DK] * (1.0 / (tok * 2 << j))

        @pl.when(is_top)
        def _():
            for c in parts_of(k):
                for j in reversed(range(nb)):
                    r_send[j, cs(c)] = lev[j, cs(c)].astype(BF16)
                top_send(nb - 1, c)

    def top_send(j, k):
        @pl.when(not_low)
        def _():
            down_copy(j, k).start()

    def relay(k):
        @pl.when(not_top)
        def _():
            for j in reversed(range(nb)):
                needed = ((z + 1) // (1 << j)) % 2 == 1
                if j == 0:
                    needed = jnp.logical_and(needed, jstar > 0)
                @pl.when(needed)
                def _(j=j):
                    down_copy(j, k).wait_recv()

                @pl.when(bit[j] == 1)
                def _(j=j):
                    came = jnp.where(j < jstar, jstar, j)
                    r_send[j, cs(k)] = (lev[j, cs(k)] + r_recv[came, cs(k)].astype(F32)).astype(BF16)
                    down_copy(j, k).start()

    def meet(k):
        @pl.when(jstar == 0)
        def _():
            down_copy(0, k).wait_recv()

        @pl.when(sends_m)
        def _():
            got = r_recv[jstar, cs(k)].astype(F32)
            own = jnp.where(odd == 1, 1.0, 0.0)
            m_send[cs(k)] = (got + own * lev1[cs(k)]).astype(BF16)
            m_copy(k).start()

    def span_grads(k):
        sc = [dot(w0g[h], hs(v_ref, h), 1, 1) for h in group(k)]
        st = [dot(hs(v_ref, h), w0g[h], 1, 1) for h in group(k)]
        for h, s, t in zip(group(k), sc, st):
            score[h] = (s * causal).astype(BF16)
            score_t[h] = (t * causal_t).astype(BF16)

    def low(f, k):
        @pl.when(low_half)
        def _():
            f(k)

    def high(f, k):
        @pl.when(high_half)
        def _():
            f(k)

    for k in range(chunks):
        level_grads(k)
        for c in parts_of(k):
            f1(c)
        if k >= 1:
            for c in parts_of(k - 1):
                low(f2, c)
    for c in parts_of(chunks - 1):
        low(f2, c)

    @pl.when(is_top)
    def _():
        for j in reversed(range(nb - 1)):
            for c in range(pieces):
                top_send(j, c)

    rest = list(range(half, heads))
    for k in range(chunks):
        for c in parts_of(k):
            relay(c)
            high(f2, c)
        span_grads(k)
        part, rest = rest[:ch], rest[ch:]
        if part:
            inside(part)

    col = lax.broadcasted_iota(jnp.int32, (tok, DK), 1)
    scales = [jnp.where(odd == 1, 1.0 / tok, 0.0)] + [1.0 / (tok * 2 << j) for j in range(nb)]
    wg = jnp.zeros((tok, DK), F32)
    for k in range(chunks):
        @pl.when(is_top)
        def _(k=k):
            for c in parts_of(k):
                for j in range(nb):
                    up_copy(j, c).wait_recv()

        cats = []
        for h in group(k):
            parts = [pair_recv[h]] + [ls[j, h] for j in range(nb)]
            cats.append(jnp.concatenate(
                [(p.astype(F32) * s).astype(BF16) for p, s in zip(parts, scales)], 1))
        los = [dot(hs(q_ref, h), c, 1, 0) for h, c in zip(group(k), cats)]
        gqs = [dot(score[h], hs(k_ref, h), 1, 0) + dot(wlg[h], c, 1, 1) for h, c in zip(group(k), cats)]
        for h, lo, gq in zip(group(k), los, gqs):
            sl = slice(h * DK, (h + 1) * DK)
            gh = hs(g_ref, h).astype(F32)
            part = intra[h]
            out = w_all[0, h] * part
            wg = jnp.where(col == h, jnp.sum(gh * part, 1, keepdims=True), wg)
            for l in range(1, levels):
                lol = lo[:, (l - 1) * DK:l * DK]
                out = out + w_all[l, h] * lol
                wg = jnp.where(col == l * heads + h, jnp.sum(gh * lol, 1, keepdims=True), wg)
            mixed_ref[:, sl] = out.astype(BF16)
            gq_ref[:, sl] = gq.astype(BF16)
        for c in parts_of(k):
            meet(c)

    lg_all[hd] = (wg.T[:rows, :] * sig).astype(BF16)
    for d in range(1, head_n):
        lg_copy(d).start()

    for k in range(chunks):
        @pl.when(gets_m)
        def _(k=k):
            for c in parts_of(k):
                m_copy(c).wait_recv()

        sgs = [(r_recv[jstar, h].astype(F32) + m_recv[h].astype(F32)).astype(BF16) for h in group(k)]
        gks = [dot(score_t[h], hs(q_ref, h), 1, 0) + dot(hs(v_ref, h), sg, 1, 1) for h, sg in zip(group(k), sgs)]
        gvs = [dot(att_t[h], w0g[h], 1, 0) + dot(hs(k_ref, h), sg, 1, 0) for h, sg in zip(group(k), sgs)]
        for h, gk, gv in zip(group(k), gks, gvs):
            sl = slice(h * DK, (h + 1) * DK)
            gk_ref[:, sl] = gk.astype(BF16)
            gv_ref[:, sl] = gv.astype(BF16)
        if k == max(chunks // 2 - 1, 0):
            for d in range(1, head_n):
                lg_wait(d)
            every = jnp.concatenate([lg_all[p] for p in range(head_n)], 0)
            ghid_ref[...] = dot(every, gatep[...], 0, 1).astype(BF16)

    for d in range(1, head_n):
        lp_copy(d).wait_send()
        lg_copy(d).wait_send()
    for k in range(pieces):
        @pl.when(sends_s)
        def _(k=k):
            pair_copy(k).wait_send()

        @pl.when(sends_m)
        def _(k=k):
            m_copy(k).wait_send()

        for j in range(nb):
            @pl.when(jnp.logical_and(not_top, ((z + 1) // (1 << j)) % 2 == 1))
            def _(j=j, k=k):
                up_copy(j, k).wait_send()

            @pl.when(jnp.logical_and(not_low, bit[j] == 1))
            def _(j=j, k=k):
                down_copy(j, k).wait_send()


def hand_over(*refs):
    n = len(refs) // 2
    sem = refs[-1]
    copies = [pltpu.make_async_copy(refs[i], refs[n + i], sem.at[i]) for i in range(n)]
    for c in copies:
        c.start()
    for c in copies:
        c.wait()


def local(seq_n, head_n, queries, keys, values, hidden, gate_weight, level_slot, out_grad):
    tok, width = queries.shape
    heads = width // DK
    levels = level_slot.shape[0]
    nb = levels - 2
    rows = heads * levels
    chunks = heads // min(SENT_HEADS, CHUNK_HEADS, heads)
    feats = hidden.shape[1]
    wide = head_n * rows
    hbm = pl.BlockSpec(memory_space=pl.ANY)
    vmem = pl.BlockSpec(memory_space=pltpu.VMEM)
    blk = (heads, DK, DK)
    sem = pltpu.SemaphoreType.DMA
    outs = [jax.ShapeDtypeStruct((tok, width), BF16)] * 4 + [
        jax.ShapeDtypeStruct((tok, feats), BF16)
    ]
    made = pl.pallas_call(
        functools.partial(mix_kernel, seq_n, head_n),
        out_shape=[pltpu.VMEM(o.shape, o.dtype) for o in outs],
        in_specs=[pl.BlockSpec(memory_space=pltpu.HBM)] * 7,
        out_specs=[vmem] * 5,
        scratch_shapes=[
            pltpu.SMEM((levels,), jnp.int32),
            pltpu.VMEM((tok, width), BF16),
            pltpu.VMEM((tok, width), BF16),
            pltpu.VMEM((tok, width), BF16),
            pltpu.VMEM((tok, feats), BF16),
            pltpu.VMEM((feats, wide), BF16),
            pltpu.VMEM((tok, width), BF16),
            pltpu.VMEM((feats, wide), BF16),
            pltpu.VMEM((head_n, rows, tok), F32),
            pltpu.VMEM((head_n - 1, rows, tok), F32),
            pltpu.VMEM((head_n, rows, tok), BF16),
            pltpu.VMEM(blk, F32),
            pltpu.VMEM(blk, BF16),
            pltpu.VMEM(blk, BF16),
            pltpu.VMEM((nb,) + blk, BF16),
            pltpu.VMEM(blk, BF16),
            pltpu.VMEM((nb,) + blk, BF16),
            pltpu.VMEM((nb + 1,) + blk, BF16),
            pltpu.VMEM(blk, BF16),
            pltpu.VMEM(blk, BF16),
            pltpu.VMEM(blk, F32),
            pltpu.VMEM((nb,) + blk, F32),
            pltpu.VMEM(blk, F32),
            pltpu.VMEM(blk, BF16),
            pltpu.VMEM(blk, BF16),
            pltpu.VMEM(blk, BF16),
            pltpu.VMEM((levels,) + blk, F32),
            pltpu.VMEM(blk, BF16),
            pltpu.VMEM((heads, tok, (levels - 1) * DK), BF16),
            sem((7,)),
            sem((head_n - 1,)), sem((head_n - 1,)),
            sem((head_n - 1,)), sem((head_n - 1,)),
            sem((chunks,)), sem((chunks,)),
            sem((nb, chunks)), sem((nb, chunks)),
            sem((nb, chunks)), sem((nb, chunks)),
            sem((chunks,)), sem((chunks,)),
        ],
        compiler_params=pltpu.CompilerParams(
            collective_id=0, has_side_effects=True, vmem_limit_bytes=VMEM_ALL
        ),
    )(level_slot, queries, keys, values, hidden, gate_weight, out_grad)
    return pl.pallas_call(
        hand_over,
        out_shape=outs,
        in_specs=[vmem] * 5,
        out_specs=[hbm] * 5,
        scratch_shapes=[sem((5,))],
    )(*made)


def solution(mesh):
    both = P("seq", "head")
    return jax.shard_map(
        functools.partial(local, mesh.shape["seq"], mesh.shape["head"]),
        mesh=mesh,
        in_specs=(both, both, both, both, P("head", None), P(), both),
        out_specs=(both,) * 5,
        check_vma=False,
    )
```

```python
import functools

import jax
import jax.numpy as jnp
from jax import lax
from jax.experimental import pallas as pl
from jax.experimental.pallas import tpu as pltpu
from jax.sharding import PartitionSpec as P

DK = 128
MESH = pl.DeviceIdType.MESH
F32 = jnp.float32
BF16 = jnp.bfloat16
CHUNK_HEADS = 2
SENT_HEADS = 1
VMEM_ALL = (64 << 20) - (1 << 21)


def dot(a, b, ca, cb):
    return lax.dot_general(a, b, (((ca,), (cb,)), ((), ())), preferred_element_type=F32)


def mix_kernel(
    seq_n, head_n,
    slot_hbm, q_hbm, k_hbm, v_hbm, hid_hbm, gate_hbm, g_hbm,
    mixed_ref, gq_ref, gk_ref, gv_ref, ghid_ref,
    slot_ref, q_ref, k_ref, v_ref, hid_ref, gate_ref, g_ref,
    gatep, lp_send, lp_recv, lg_all,
    s_f32, s_bf, pair_recv, ls, h_send, r_send, r_recv, m_send, m_recv,
    intra, lev, lev1, att_t, score, score_t, w_all, w0g, wlg,
    in_sem,
    lp_ss, lp_rs, lg_ss, lg_rs, pr_ss, pr_rs, up_ss, up_rs, dn_ss, dn_rs, m_ss, m_rs,
):
    tok = q_ref.shape[0]
    heads = q_ref.shape[1] // DK
    levels = lev.shape[0] + 2
    nb = levels - 2
    rows = heads * levels
    ch = min(CHUNK_HEADS, heads)
    chunks = heads // ch
    sent = min(SENT_HEADS, ch)
    pieces = heads // sent
    zn = seq_n // 2

    loads = [
        pltpu.make_async_copy(src, dst, in_sem.at[i])
        for i, (src, dst) in enumerate(
            [(gate_hbm, gate_ref), (hid_hbm, hid_ref), (k_hbm, k_ref), (v_hbm, v_ref),
             (q_hbm, q_ref), (g_hbm, g_ref), (slot_hbm, slot_ref)]
        )
    ]
    for c in loads[6:] + loads[:6]:
        c.start()

    me = lax.axis_index("seq")
    hd = lax.axis_index("head")
    odd = me % 2
    z = me // 2
    pair = me + 1 - 2 * odd
    above = jnp.minimum(z + 1, zn - 1) * 2 + odd
    below = jnp.maximum(z - 1, 0) * 2 + odd
    is_top = z == zn - 1
    not_top = z < zn - 1
    not_low = z > 0
    low_half = z < zn // 2
    high_half = z >= zn // 2
    bit = [(z // (1 << j)) % 2 for j in range(nb)]
    jstar = jnp.int32(nb)
    for j in reversed(range(nb)):
        jstar = jnp.where(bit[j] == 0, j, jstar)
    peers = [lax.rem(hd + d, head_n) for d in range(1, head_n)]

    barrier = pltpu.get_barrier_semaphore()
    pl.semaphore_signal(barrier, inc=1, device_id={"seq": pair}, device_id_type=MESH)
    for p in peers:
        pl.semaphore_signal(barrier, inc=1, device_id={"head": p}, device_id_type=MESH)

    @pl.when(not_top)
    def _():
        pl.semaphore_signal(barrier, inc=1, device_id={"seq": above}, device_id_type=MESH)

    @pl.when(not_low)
    def _():
        pl.semaphore_signal(barrier, inc=1, device_id={"seq": below}, device_id_type=MESH)

    def cs(k):
        return pl.ds(k * sent, sent)

    def parts_of(k):
        return range(k * ch // sent, (k + 1) * ch // sent)

    def group(k):
        return range(k * ch, (k + 1) * ch)

    def copy(src, dst, ss, rs, where):
        return pltpu.make_async_remote_copy(
            src_ref=src, dst_ref=dst, send_sem=ss, recv_sem=rs, device_id=where, device_id_type=MESH
        )

    def lp_copy(d):
        return copy(
            lp_send.at[peers[d - 1]], lp_recv.at[d - 1], lp_ss.at[d - 1], lp_rs.at[d - 1],
            {"head": peers[d - 1]},
        )

    def lg_copy(d):
        return copy(
            lg_all.at[hd], lg_all.at[hd], lg_ss.at[d - 1], lg_rs.at[d - 1], {"head": peers[d - 1]}
        )

    def lg_wait(d):
        src = lax.rem(hd + head_n - d, head_n)
        copy(lg_all.at[src], lg_all.at[src], lg_ss.at[d - 1], lg_rs.at[d - 1], {"head": peers[d - 1]}).wait_recv()

    def pair_copy(k):
        return copy(s_bf.at[cs(k)], pair_recv.at[cs(k)], pr_ss.at[k], pr_rs.at[k], {"seq": pair})

    def up_copy(j, k):
        return copy(ls.at[j, cs(k)], ls.at[j, cs(k)], up_ss.at[j, k], up_rs.at[j, k], {"seq": above})

    def h_copy(k):
        j = jnp.minimum(jstar, nb - 1)
        return copy(h_send.at[cs(k)], ls.at[j, cs(k)], up_ss.at[j, k], up_rs.at[j, k], {"seq": above})

    def down_copy(j, k):
        return copy(r_send.at[j, cs(k)], r_recv.at[j, cs(k)], dn_ss.at[j, k], dn_rs.at[j, k], {"seq": below})

    def m_copy(k):
        return copy(m_send.at[cs(k)], m_recv.at[cs(k)], m_ss.at[k], m_rs.at[k], {"seq": pair})

    def hs(ref, h):
        return ref[:, h * DK:(h + 1) * DK]

    wide = head_n * rows
    r_from = lax.broadcasted_iota(jnp.int32, (wide, wide), 0)
    r_to = lax.broadcasted_iota(jnp.int32, (1, wide), 1)
    in_dev = r_to % rows
    loads[6].wait()
    lev_of = in_dev // heads
    slot_of = jnp.zeros((1, wide), jnp.int32)
    for l in range(levels):
        slot_of = jnp.where(lev_of == l, slot_ref[l], slot_of)
    target = (r_to // rows) * rows + (in_dev % heads) * levels + slot_of
    perm = jnp.where(r_from == target, 1.0, 0.0).astype(BF16)
    loads[0].wait()
    loads[1].wait()
    gatep[...] = dot(gate_ref[...], perm, 1, 0).astype(BF16)
    partial = dot(hid_ref[...], gatep[...], 1, 0).T
    for p in range(head_n):
        lp_send[p] = partial[p * rows:(p + 1) * rows, :]

    loads[2].wait()
    loads[3].wait()

    def states(hh):
        for h in hh:
            s = dot(hs(k_ref, h), hs(v_ref, h), 0, 0)
            s_f32[h] = s
            s_bf[h] = s.astype(BF16)

    states(group(0))

    pl.semaphore_wait(
        barrier, head_n + jnp.where(not_top, 1, 0) + jnp.where(not_low, 1, 0)
    )
    for d in range(1, head_n):
        lp_copy(d).start()

    sends_s = jnp.logical_or(odd == 0, not_top)
    gets_s = jnp.logical_or(odd == 1, not_top)
    sends_m = jnp.logical_or(odd == 1, not_top)
    gets_m = jnp.logical_or(odd == 0, not_top)

    def send_pair(k):
        @pl.when(sends_s)
        def _():
            pair_copy(k).start()

    for c in parts_of(0):
        send_pair(c)
    states(range(ch, heads))
    for k in range(1, chunks):
        for c in parts_of(k):
            send_pair(c)

    for j in range(nb):
        @pl.when(bit[j] == 0)
        def _(j=j):
            ls[j] = jnp.zeros(ls.shape[1:], BF16)

    r_recv[nb] = jnp.zeros(r_recv.shape[1:], BF16)

    @pl.when(jnp.logical_and(is_top, odd == 0))
    def _():
        pair_recv[...] = jnp.zeros(pair_recv.shape, BF16)

    @pl.when(jnp.logical_and(is_top, odd == 1))
    def _():
        m_recv[...] = jnp.zeros(m_recv.shape, BF16)

    t_pos = lax.broadcasted_iota(jnp.int32, (tok, tok), 0)
    s_pos = lax.broadcasted_iota(jnp.int32, (tok, tok), 1)
    causal = jnp.where(t_pos >= s_pos, 1.0 / tok, 0.0)
    causal_t = jnp.where(s_pos >= t_pos, 1.0 / tok, 0.0)

    def inside(hh):
        sc = [dot(hs(q_ref, h), hs(k_ref, h), 1, 1) for h in hh]
        st = [dot(hs(k_ref, h), hs(q_ref, h), 1, 1) for h in hh]
        at = [(s * causal).astype(BF16) for s in sc]
        for h, s in zip(hh, st):
            att_t[h] = (s * causal_t).astype(BF16)
        for h, a in zip(hh, at):
            intra[h] = dot(a, hs(v_ref, h), 1, 0)

    def f1(k):
        @pl.when(gets_s)
        def _():
            pair_copy(k).wait_recv()

        @pl.when(jnp.logical_and(not_top, jstar == 0))
        def _():
            h_send[cs(k)] = (s_f32[cs(k)] + pair_recv[cs(k)].astype(F32)).astype(BF16)
            h_copy(k).start()

    def f2(k):
        @pl.when(not_top)
        def _():
            for j in range(nb):
                @pl.when(bit[j] == 1)
                def _(j=j):
                    up_copy(j, k).wait_recv()

            for j in range(nb):
                @pl.when(jnp.logical_and(bit[j] == 1, j > jstar))
                def _(j=j):
                    up_copy(j, k).start()

            @pl.when(jstar > 0)
            def _():
                total = s_f32[cs(k)] + pair_recv[cs(k)].astype(F32)
                for j in range(nb):
                    total = total + jnp.where(j < jstar, ls[j, cs(k)].astype(F32), 0.0)
                h_send[cs(k)] = total.astype(BF16)
                h_copy(k).start()

    loads[4].wait()
    half = max(heads // 2, 1)
    inside(range(half))
    loads[5].wait()

    mine = lp_send[hd]
    for d in range(1, head_n):
        lp_copy(d).wait_recv()
    for d in range(1, head_n):
        mine = mine + lp_recv[d - 1]
    soft = jnp.maximum(mine, 0.0) + jnp.log1p(jnp.exp(-jnp.abs(mine)))
    pad = jnp.zeros((DK - rows, tok), F32)
    soft_t = jnp.concatenate([soft, pad], 0).T if rows < DK else soft.T
    sig = jax.nn.sigmoid(mine)

    def weigh(k):
        for h in group(k):
            gh = hs(g_ref, h).astype(F32)
            for l in range(levels):
                c = l * heads + h
                w = jnp.broadcast_to(soft_t[:, c:c + 1], (tok, DK))
                w_all[l, h] = w
                if l == 0:
                    w0g[h] = (w * gh).astype(BF16)
                else:
                    wlg[h, :, (l - 1) * DK:l * DK] = (w * gh).astype(BF16)

    def level_grads(k):
        weigh(k)
        for h in group(k):
            grads = dot(hs(q_ref, h), wlg[h], 0, 0)
            lev1[h] = grads[:, :DK] * (1.0 / tok)
            for j in range(nb):
                lev[j, h] = grads[:, (j + 1) * DK:(j + 2) * DK] * (1.0 / (tok * 2 << j))

        @pl.when(is_top)
        def _():
            for c in parts_of(k):
                for j in reversed(range(nb)):
                    r_send[j, cs(c)] = lev[j, cs(c)].astype(BF16)
                top_send(nb - 1, c)

    def top_send(j, k):
        @pl.when(not_low)
        def _():
            down_copy(j, k).start()

    def relay(k):
        @pl.when(not_top)
        def _():
            for j in reversed(range(nb)):
                needed = ((z + 1) // (1 << j)) % 2 == 1
                if j == 0:
                    needed = jnp.logical_and(needed, jstar > 0)
                @pl.when(needed)
                def _(j=j):
                    down_copy(j, k).wait_recv()

                @pl.when(bit[j] == 1)
                def _(j=j):
                    came = jnp.where(j < jstar, jstar, j)
                    r_send[j, cs(k)] = (lev[j, cs(k)] + r_recv[came, cs(k)].astype(F32)).astype(BF16)
                    down_copy(j, k).start()

    def meet(k):
        @pl.when(jstar == 0)
        def _():
            down_copy(0, k).wait_recv()

        @pl.when(sends_m)
        def _():
            got = r_recv[jstar, cs(k)].astype(F32)
            own = jnp.where(odd == 1, 1.0, 0.0)
            m_send[cs(k)] = (got + own * lev1[cs(k)]).astype(BF16)
            m_copy(k).start()

    def span_grads(k):
        sc = [dot(w0g[h], hs(v_ref, h), 1, 1) for h in group(k)]
        st = [dot(hs(v_ref, h), w0g[h], 1, 1) for h in group(k)]
        for h, s, t in zip(group(k), sc, st):
            score[h] = (s * causal).astype(BF16)
            score_t[h] = (t * causal_t).astype(BF16)

    def low(f, k):
        @pl.when(low_half)
        def _():
            f(k)

    def high(f, k):
        @pl.when(high_half)
        def _():
            f(k)

    for k in range(chunks):
        level_grads(k)
        for c in parts_of(k):
            f1(c)
        if k >= 1:
            for c in parts_of(k - 1):
                low(f2, c)
    for c in parts_of(chunks - 1):
        low(f2, c)

    @pl.when(is_top)
    def _():
        for j in reversed(range(nb - 1)):
            for c in range(pieces):
                top_send(j, c)

    rest = list(range(half, heads))
    for k in range(chunks):
        for c in parts_of(k):
            relay(c)
            high(f2, c)
        span_grads(k)
        part, rest = rest[:ch], rest[ch:]
        if part:
            inside(part)

    col = lax.broadcasted_iota(jnp.int32, (tok, DK), 1)
    scales = [jnp.where(odd == 1, 1.0 / tok, 0.0)] + [1.0 / (tok * 2 << j) for j in range(nb)]
    wg = jnp.zeros((tok, DK), F32)
    for k in range(chunks):
        @pl.when(is_top)
        def _(k=k):
            for c in parts_of(k):
                for j in range(nb):
                    up_copy(j, c).wait_recv()

        cats = []
        for h in group(k):
            parts = [pair_recv[h]] + [ls[j, h] for j in range(nb)]
            cats.append(jnp.concatenate(
                [(p.astype(F32) * s).astype(BF16) for p, s in zip(parts, scales)], 1))
        los = [dot(hs(q_ref, h), c, 1, 0) for h, c in zip(group(k), cats)]
        gqs = [dot(score[h], hs(k_ref, h), 1, 0) + dot(wlg[h], c, 1, 1) for h, c in zip(group(k), cats)]
        for h, lo, gq in zip(group(k), los, gqs):
            sl = slice(h * DK, (h + 1) * DK)
            gh = hs(g_ref, h).astype(F32)
            part = intra[h]
            out = w_all[0, h] * part
            wg = jnp.where(col == h, jnp.sum(gh * part, 1, keepdims=True), wg)
            for l in range(1, levels):
                lol = lo[:, (l - 1) * DK:l * DK]
                out = out + w_all[l, h] * lol
                wg = jnp.where(col == l * heads + h, jnp.sum(gh * lol, 1, keepdims=True), wg)
            mixed_ref[:, sl] = out.astype(BF16)
            gq_ref[:, sl] = gq.astype(BF16)
        for c in parts_of(k):
            meet(c)

    lg_all[hd] = (wg.T[:rows, :] * sig).astype(BF16)
    for d in range(1, head_n):
        lg_copy(d).start()

    for k in range(chunks):
        @pl.when(gets_m)
        def _(k=k):
            for c in parts_of(k):
                m_copy(c).wait_recv()

        sgs = [(r_recv[jstar, h].astype(F32) + m_recv[h].astype(F32)).astype(BF16) for h in group(k)]
        gks = [dot(score_t[h], hs(q_ref, h), 1, 0) + dot(hs(v_ref, h), sg, 1, 1) for h, sg in zip(group(k), sgs)]
        gvs = [dot(att_t[h], w0g[h], 1, 0) + dot(hs(k_ref, h), sg, 1, 0) for h, sg in zip(group(k), sgs)]
        for h, gk, gv in zip(group(k), gks, gvs):
            sl = slice(h * DK, (h + 1) * DK)
            gk_ref[:, sl] = gk.astype(BF16)
            gv_ref[:, sl] = gv.astype(BF16)
        if k == max(chunks // 2 - 1, 0):
            for d in range(1, head_n):
                lg_wait(d)
            every = jnp.concatenate([lg_all[p] for p in range(head_n)], 0)
            ghid_ref[...] = dot(every, gatep[...], 0, 1).astype(BF16)

    for d in range(1, head_n):
        lp_copy(d).wait_send()
        lg_copy(d).wait_send()
    for k in range(pieces):
        @pl.when(sends_s)
        def _(k=k):
            pair_copy(k).wait_send()

        @pl.when(sends_m)
        def _(k=k):
            m_copy(k).wait_send()

        for j in range(nb):
            @pl.when(jnp.logical_and(not_top, ((z + 1) // (1 << j)) % 2 == 1))
            def _(j=j, k=k):
                up_copy(j, k).wait_send()

            @pl.when(jnp.logical_and(not_low, bit[j] == 1))
            def _(j=j, k=k):
                down_copy(j, k).wait_send()


def hand_over(*refs):
    n = len(refs) // 2
    sem = refs[-1]
    copies = [pltpu.make_async_copy(refs[i], refs[n + i], sem.at[i]) for i in range(n)]
    for c in copies:
        c.start()
    for c in copies:
        c.wait()


def local(seq_n, head_n, queries, keys, values, hidden, gate_weight, level_slot, out_grad):
    tok, width = queries.shape
    heads = width // DK
    levels = level_slot.shape[0]
    nb = levels - 2
    rows = heads * levels
    chunks = heads // min(SENT_HEADS, CHUNK_HEADS, heads)
    feats = hidden.shape[1]
    wide = head_n * rows
    hbm = pl.BlockSpec(memory_space=pl.ANY)
    vmem = pl.BlockSpec(memory_space=pltpu.VMEM)
    blk = (heads, DK, DK)
    sem = pltpu.SemaphoreType.DMA
    outs = [jax.ShapeDtypeStruct((tok, width), BF16)] * 4 + [
        jax.ShapeDtypeStruct((tok, feats), BF16)
    ]
    made = pl.pallas_call(
        functools.partial(mix_kernel, seq_n, head_n),
        out_shape=[pltpu.VMEM(o.shape, o.dtype) for o in outs],
        in_specs=[pl.BlockSpec(memory_space=pltpu.HBM)] * 7,
        out_specs=[vmem] * 5,
        scratch_shapes=[
            pltpu.SMEM((levels,), jnp.int32),
            pltpu.VMEM((tok, width), BF16),
            pltpu.VMEM((tok, width), BF16),
            pltpu.VMEM((tok, width), BF16),
            pltpu.VMEM((tok, feats), BF16),
            pltpu.VMEM((feats, wide), BF16),
            pltpu.VMEM((tok, width), BF16),
            pltpu.VMEM((feats, wide), BF16),
            pltpu.VMEM((head_n, rows, tok), F32),
            pltpu.VMEM((head_n - 1, rows, tok), F32),
            pltpu.VMEM((head_n, rows, tok), BF16),
            pltpu.VMEM(blk, F32),
            pltpu.VMEM(blk, BF16),
            pltpu.VMEM(blk, BF16),
            pltpu.VMEM((nb,) + blk, BF16),
            pltpu.VMEM(blk, BF16),
            pltpu.VMEM((nb,) + blk, BF16),
            pltpu.VMEM((nb + 1,) + blk, BF16),
            pltpu.VMEM(blk, BF16),
            pltpu.VMEM(blk, BF16),
            pltpu.VMEM(blk, F32),
            pltpu.VMEM((nb,) + blk, F32),
            pltpu.VMEM(blk, F32),
            pltpu.VMEM(blk, BF16),
            pltpu.VMEM(blk, BF16),
            pltpu.VMEM(blk, BF16),
            pltpu.VMEM((levels,) + blk, F32),
            pltpu.VMEM(blk, BF16),
            pltpu.VMEM((heads, tok, (levels - 1) * DK), BF16),
            sem((7,)),
            sem((head_n - 1,)), sem((head_n - 1,)),
            sem((head_n - 1,)), sem((head_n - 1,)),
            sem((chunks,)), sem((chunks,)),
            sem((nb, chunks)), sem((nb, chunks)),
            sem((nb, chunks)), sem((nb, chunks)),
            sem((chunks,)), sem((chunks,)),
        ],
        compiler_params=pltpu.CompilerParams(
            collective_id=0, has_side_effects=True, vmem_limit_bytes=VMEM_ALL
        ),
    )(level_slot, queries, keys, values, hidden, gate_weight, out_grad)
    return pl.pallas_call(
        hand_over,
        out_shape=outs,
        in_specs=[hbm] * 5,
        out_specs=[hbm] * 5,
        scratch_shapes=[sem((5,))],
        compiler_params=pltpu.CompilerParams(vmem_limit_bytes=4 << 20),
    )(*made)


def solution(mesh):
    both = P("seq", "head")
    return jax.shard_map(
        functools.partial(local, mesh.shape["seq"], mesh.shape["head"]),
        mesh=mesh,
        in_specs=(both, both, both, both, P("head", None), P(), both),
        out_specs=(both,) * 5,
        check_vma=False,
    )
```

```python
import functools

import jax
import jax.numpy as jnp
from jax import lax
from jax.experimental import pallas as pl
from jax.experimental.pallas import tpu as pltpu
from jax.sharding import PartitionSpec as P

DK = 128
MESH = pl.DeviceIdType.MESH
F32 = jnp.float32
BF16 = jnp.bfloat16
CHUNK_HEADS = 4
SENT_HEADS = 1
VMEM_ALL = (64 << 20) - (1 << 21)


def dot(a, b, ca, cb):
    return lax.dot_general(a, b, (((ca,), (cb,)), ((), ())), preferred_element_type=F32)


def mix_kernel(
    seq_n, head_n,
    slot_hbm, q_hbm, k_hbm, v_hbm, hid_hbm, gate_hbm, g_hbm,
    mixed_ref, gq_ref, gk_ref, gv_ref, ghid_ref,
    slot_ref, q_ref, k_ref, v_ref, hid_ref, gate_ref, g_ref,
    gatep, lp_send, lp_recv, lg_all,
    s_f32, s_bf, pair_recv, ls, h_send, r_send, r_recv, m_send, m_recv,
    intra, lev, lev1, att_t, score, score_t, w_all, w0g, wlg,
    in_sem,
    lp_ss, lp_rs, lg_ss, lg_rs, pr_ss, pr_rs, up_ss, up_rs, dn_ss, dn_rs, m_ss, m_rs,
):
    tok = q_ref.shape[0]
    heads = q_ref.shape[1] // DK
    levels = lev.shape[0] + 2
    nb = levels - 2
    rows = heads * levels
    ch = min(CHUNK_HEADS, heads)
    chunks = heads // ch
    sent = min(SENT_HEADS, ch)
    pieces = heads // sent
    zn = seq_n // 2

    loads = [
        pltpu.make_async_copy(src, dst, in_sem.at[i])
        for i, (src, dst) in enumerate(
            [(gate_hbm, gate_ref), (hid_hbm, hid_ref), (k_hbm, k_ref), (v_hbm, v_ref),
             (q_hbm, q_ref), (g_hbm, g_ref), (slot_hbm, slot_ref)]
        )
    ]
    for c in loads[6:] + loads[:6]:
        c.start()

    me = lax.axis_index("seq")
    hd = lax.axis_index("head")
    odd = me % 2
    z = me // 2
    pair = me + 1 - 2 * odd
    above = jnp.minimum(z + 1, zn - 1) * 2 + odd
    below = jnp.maximum(z - 1, 0) * 2 + odd
    is_top = z == zn - 1
    not_top = z < zn - 1
    not_low = z > 0
    low_half = z < zn // 2
    high_half = z >= zn // 2
    bit = [(z // (1 << j)) % 2 for j in range(nb)]
    jstar = jnp.int32(nb)
    for j in reversed(range(nb)):
        jstar = jnp.where(bit[j] == 0, j, jstar)
    peers = [lax.rem(hd + d, head_n) for d in range(1, head_n)]

    barrier = pltpu.get_barrier_semaphore()
    pl.semaphore_signal(barrier, inc=1, device_id={"seq": pair}, device_id_type=MESH)
    for p in peers:
        pl.semaphore_signal(barrier, inc=1, device_id={"head": p}, device_id_type=MESH)

    @pl.when(not_top)
    def _():
        pl.semaphore_signal(barrier, inc=1, device_id={"seq": above}, device_id_type=MESH)

    @pl.when(not_low)
    def _():
        pl.semaphore_signal(barrier, inc=1, device_id={"seq": below}, device_id_type=MESH)

    def cs(k):
        return pl.ds(k * sent, sent)

    def parts_of(k):
        return range(k * ch // sent, (k + 1) * ch // sent)

    def group(k):
        return range(k * ch, (k + 1) * ch)

    def copy(src, dst, ss, rs, where):
        return pltpu.make_async_remote_copy(
            src_ref=src, dst_ref=dst, send_sem=ss, recv_sem=rs, device_id=where, device_id_type=MESH
        )

    def lp_copy(d):
        return copy(
            lp_send.at[peers[d - 1]], lp_recv.at[d - 1], lp_ss.at[d - 1], lp_rs.at[d - 1],
            {"head": peers[d - 1]},
        )

    def lg_copy(d):
        return copy(
            lg_all.at[hd], lg_all.at[hd], lg_ss.at[d - 1], lg_rs.at[d - 1], {"head": peers[d - 1]}
        )

    def lg_wait(d):
        src = lax.rem(hd + head_n - d, head_n)
        copy(lg_all.at[src], lg_all.at[src], lg_ss.at[d - 1], lg_rs.at[d - 1], {"head": peers[d - 1]}).wait_recv()

    def pair_copy(k):
        return copy(s_bf.at[cs(k)], pair_recv.at[cs(k)], pr_ss.at[k], pr_rs.at[k], {"seq": pair})

    def up_copy(j, k):
        return copy(ls.at[j, cs(k)], ls.at[j, cs(k)], up_ss.at[j, k], up_rs.at[j, k], {"seq": above})

    def h_copy(k):
        j = jnp.minimum(jstar, nb - 1)
        return copy(h_send.at[cs(k)], ls.at[j, cs(k)], up_ss.at[j, k], up_rs.at[j, k], {"seq": above})

    def down_copy(j, k):
        return copy(r_send.at[j, cs(k)], r_recv.at[j, cs(k)], dn_ss.at[j, k], dn_rs.at[j, k], {"seq": below})

    def m_copy(k):
        return copy(m_send.at[cs(k)], m_recv.at[cs(k)], m_ss.at[k], m_rs.at[k], {"seq": pair})

    def hs(ref, h):
        return ref[:, h * DK:(h + 1) * DK]

    wide = head_n * rows
    r_from = lax.broadcasted_iota(jnp.int32, (wide, wide), 0)
    r_to = lax.broadcasted_iota(jnp.int32, (1, wide), 1)
    in_dev = r_to % rows
    loads[6].wait()
    lev_of = in_dev // heads
    slot_of = jnp.zeros((1, wide), jnp.int32)
    for l in range(levels):
        slot_of = jnp.where(lev_of == l, slot_ref[l], slot_of)
    target = (r_to // rows) * rows + (in_dev % heads) * levels + slot_of
    perm = jnp.where(r_from == target, 1.0, 0.0).astype(BF16)
    loads[0].wait()
    loads[1].wait()
    gatep[...] = dot(gate_ref[...], perm, 1, 0).astype(BF16)
    partial = dot(hid_ref[...], gatep[...], 1, 0).T
    for p in range(head_n):
        lp_send[p] = partial[p * rows:(p + 1) * rows, :]

    loads[2].wait()
    loads[3].wait()

    def states(hh):
        for h in hh:
            s = dot(hs(k_ref, h), hs(v_ref, h), 0, 0)
            s_f32[h] = s
            s_bf[h] = s.astype(BF16)

    states(group(0))

    pl.semaphore_wait(
        barrier, head_n + jnp.where(not_top, 1, 0) + jnp.where(not_low, 1, 0)
    )
    for d in range(1, head_n):
        lp_copy(d).start()

    sends_s = jnp.logical_or(odd == 0, not_top)
    gets_s = jnp.logical_or(odd == 1, not_top)
    sends_m = jnp.logical_or(odd == 1, not_top)
    gets_m = jnp.logical_or(odd == 0, not_top)

    def send_pair(k):
        @pl.when(sends_s)
        def _():
            pair_copy(k).start()

    for c in parts_of(0):
        send_pair(c)
    states(range(ch, heads))
    for k in range(1, chunks):
        for c in parts_of(k):
            send_pair(c)

    for j in range(nb):
        @pl.when(bit[j] == 0)
        def _(j=j):
            ls[j] = jnp.zeros(ls.shape[1:], BF16)

    r_recv[nb] = jnp.zeros(r_recv.shape[1:], BF16)

    @pl.when(jnp.logical_and(is_top, odd == 0))
    def _():
        pair_recv[...] = jnp.zeros(pair_recv.shape, BF16)

    @pl.when(jnp.logical_and(is_top, odd == 1))
    def _():
        m_recv[...] = jnp.zeros(m_recv.shape, BF16)

    t_pos = lax.broadcasted_iota(jnp.int32, (tok, tok), 0)
    s_pos = lax.broadcasted_iota(jnp.int32, (tok, tok), 1)
    causal = jnp.where(t_pos >= s_pos, 1.0 / tok, 0.0)
    causal_t = jnp.where(s_pos >= t_pos, 1.0 / tok, 0.0)

    def inside(hh):
        sc = [dot(hs(q_ref, h), hs(k_ref, h), 1, 1) for h in hh]
        st = [dot(hs(k_ref, h), hs(q_ref, h), 1, 1) for h in hh]
        at = [(s * causal).astype(BF16) for s in sc]
        for h, s in zip(hh, st):
            att_t[h] = (s * causal_t).astype(BF16)
        for h, a in zip(hh, at):
            intra[h] = dot(a, hs(v_ref, h), 1, 0)

    def f1(k):
        @pl.when(gets_s)
        def _():
            pair_copy(k).wait_recv()

        @pl.when(jnp.logical_and(not_top, jstar == 0))
        def _():
            h_send[cs(k)] = (s_f32[cs(k)] + pair_recv[cs(k)].astype(F32)).astype(BF16)
            h_copy(k).start()

    def f2(k):
        @pl.when(not_top)
        def _():
            for j in range(nb):
                @pl.when(bit[j] == 1)
                def _(j=j):
                    up_copy(j, k).wait_recv()

            for j in range(nb):
                @pl.when(jnp.logical_and(bit[j] == 1, j > jstar))
                def _(j=j):
                    up_copy(j, k).start()

            @pl.when(jstar > 0)
            def _():
                total = s_f32[cs(k)] + pair_recv[cs(k)].astype(F32)
                for j in range(nb):
                    total = total + jnp.where(j < jstar, ls[j, cs(k)].astype(F32), 0.0)
                h_send[cs(k)] = total.astype(BF16)
                h_copy(k).start()

    loads[4].wait()
    half = max(heads // 2, 1)
    inside(range(half))
    loads[5].wait()

    mine = lp_send[hd]
    for d in range(1, head_n):
        lp_copy(d).wait_recv()
    for d in range(1, head_n):
        mine = mine + lp_recv[d - 1]
    soft = jnp.maximum(mine, 0.0) + jnp.log1p(jnp.exp(-jnp.abs(mine)))
    pad = jnp.zeros((DK - rows, tok), F32)
    soft_t = jnp.concatenate([soft, pad], 0).T if rows < DK else soft.T
    sig = jax.nn.sigmoid(mine)

    def weigh(k):
        for h in group(k):
            gh = hs(g_ref, h).astype(F32)
            for l in range(levels):
                c = l * heads + h
                w = jnp.broadcast_to(soft_t[:, c:c + 1], (tok, DK))
                w_all[l, h] = w
                if l == 0:
                    w0g[h] = (w * gh).astype(BF16)
                else:
                    wlg[h, :, (l - 1) * DK:l * DK] = (w * gh).astype(BF16)

    def level_grads(k):
        weigh(k)
        for h in group(k):
            grads = dot(hs(q_ref, h), wlg[h], 0, 0)
            lev1[h] = grads[:, :DK] * (1.0 / tok)
            for j in range(nb):
                lev[j, h] = grads[:, (j + 1) * DK:(j + 2) * DK] * (1.0 / (tok * 2 << j))

        @pl.when(is_top)
        def _():
            for c in parts_of(k):
                for j in reversed(range(nb)):
                    r_send[j, cs(c)] = lev[j, cs(c)].astype(BF16)
                top_send(nb - 1, c)

    def top_send(j, k):
        @pl.when(not_low)
        def _():
            down_copy(j, k).start()

    def relay(k):
        @pl.when(not_top)
        def _():
            for j in reversed(range(nb)):
                needed = ((z + 1) // (1 << j)) % 2 == 1
                if j == 0:
                    needed = jnp.logical_and(needed, jstar > 0)
                @pl.when(needed)
                def _(j=j):
                    down_copy(j, k).wait_recv()

                @pl.when(bit[j] == 1)
                def _(j=j):
                    came = jnp.where(j < jstar, jstar, j)
                    r_send[j, cs(k)] = (lev[j, cs(k)] + r_recv[came, cs(k)].astype(F32)).astype(BF16)
                    down_copy(j, k).start()

    def meet(k):
        @pl.when(jstar == 0)
        def _():
            down_copy(0, k).wait_recv()

        @pl.when(sends_m)
        def _():
            got = r_recv[jstar, cs(k)].astype(F32)
            own = jnp.where(odd == 1, 1.0, 0.0)
            m_send[cs(k)] = (got + own * lev1[cs(k)]).astype(BF16)
            m_copy(k).start()

    def span_grads(k):
        sc = [dot(w0g[h], hs(v_ref, h), 1, 1) for h in group(k)]
        st = [dot(hs(v_ref, h), w0g[h], 1, 1) for h in group(k)]
        for h, s, t in zip(group(k), sc, st):
            score[h] = (s * causal).astype(BF16)
            score_t[h] = (t * causal_t).astype(BF16)

    def low(f, k):
        @pl.when(low_half)
        def _():
            f(k)

    def high(f, k):
        @pl.when(high_half)
        def _():
            f(k)

    for k in range(chunks):
        level_grads(k)
        for c in parts_of(k):
            f1(c)
        if k >= 1:
            for c in parts_of(k - 1):
                low(f2, c)
    for c in parts_of(chunks - 1):
        low(f2, c)

    @pl.when(is_top)
    def _():
        for j in reversed(range(nb - 1)):
            for c in range(pieces):
                top_send(j, c)

    rest = list(range(half, heads))
    for k in range(chunks):
        for c in parts_of(k):
            relay(c)
            high(f2, c)
        span_grads(k)
        part, rest = rest[:ch], rest[ch:]
        if part:
            inside(part)

    col = lax.broadcasted_iota(jnp.int32, (tok, DK), 1)
    scales = [jnp.where(odd == 1, 1.0 / tok, 0.0)] + [1.0 / (tok * 2 << j) for j in range(nb)]
    wg = jnp.zeros((tok, DK), F32)
    for k in range(chunks):
        @pl.when(is_top)
        def _(k=k):
            for c in parts_of(k):
                for j in range(nb):
                    up_copy(j, c).wait_recv()

        cats = []
        for h in group(k):
            parts = [pair_recv[h]] + [ls[j, h] for j in range(nb)]
            cats.append(jnp.concatenate(
                [(p.astype(F32) * s).astype(BF16) for p, s in zip(parts, scales)], 1))
        los = [dot(hs(q_ref, h), c, 1, 0) for h, c in zip(group(k), cats)]
        gqs = [dot(score[h], hs(k_ref, h), 1, 0) + dot(wlg[h], c, 1, 1) for h, c in zip(group(k), cats)]
        for h, lo, gq in zip(group(k), los, gqs):
            sl = slice(h * DK, (h + 1) * DK)
            gh = hs(g_ref, h).astype(F32)
            part = intra[h]
            out = w_all[0, h] * part
            wg = jnp.where(col == h, jnp.sum(gh * part, 1, keepdims=True), wg)
            for l in range(1, levels):
                lol = lo[:, (l - 1) * DK:l * DK]
                out = out + w_all[l, h] * lol
                wg = jnp.where(col == l * heads + h, jnp.sum(gh * lol, 1, keepdims=True), wg)
            mixed_ref[:, sl] = out.astype(BF16)
            gq_ref[:, sl] = gq.astype(BF16)
        for c in parts_of(k):
            meet(c)

    lg_all[hd] = (wg.T[:rows, :] * sig).astype(BF16)
    for d in range(1, head_n):
        lg_copy(d).start()

    for k in range(chunks):
        @pl.when(gets_m)
        def _(k=k):
            for c in parts_of(k):
                m_copy(c).wait_recv()

        sgs = [(r_recv[jstar, h].astype(F32) + m_recv[h].astype(F32)).astype(BF16) for h in group(k)]
        gks = [dot(score_t[h], hs(q_ref, h), 1, 0) + dot(hs(v_ref, h), sg, 1, 1) for h, sg in zip(group(k), sgs)]
        gvs = [dot(att_t[h], w0g[h], 1, 0) + dot(hs(k_ref, h), sg, 1, 0) for h, sg in zip(group(k), sgs)]
        for h, gk, gv in zip(group(k), gks, gvs):
            sl = slice(h * DK, (h + 1) * DK)
            gk_ref[:, sl] = gk.astype(BF16)
            gv_ref[:, sl] = gv.astype(BF16)
        if k == max(chunks // 2 - 1, 0):
            for d in range(1, head_n):
                lg_wait(d)
            every = jnp.concatenate([lg_all[p] for p in range(head_n)], 0)
            ghid_ref[...] = dot(every, gatep[...], 0, 1).astype(BF16)

    for d in range(1, head_n):
        lp_copy(d).wait_send()
        lg_copy(d).wait_send()
    for k in range(pieces):
        @pl.when(sends_s)
        def _(k=k):
            pair_copy(k).wait_send()

        @pl.when(sends_m)
        def _(k=k):
            m_copy(k).wait_send()

        for j in range(nb):
            @pl.when(jnp.logical_and(not_top, ((z + 1) // (1 << j)) % 2 == 1))
            def _(j=j, k=k):
                up_copy(j, k).wait_send()

            @pl.when(jnp.logical_and(not_low, bit[j] == 1))
            def _(j=j, k=k):
                down_copy(j, k).wait_send()


def hand_over(*refs):
    n = len(refs) // 2
    sem = refs[-1]
    copies = [pltpu.make_async_copy(refs[i], refs[n + i], sem.at[i]) for i in range(n)]
    for c in copies:
        c.start()
    for c in copies:
        c.wait()


def local(seq_n, head_n, queries, keys, values, hidden, gate_weight, level_slot, out_grad):
    tok, width = queries.shape
    heads = width // DK
    levels = level_slot.shape[0]
    nb = levels - 2
    rows = heads * levels
    chunks = heads // min(SENT_HEADS, CHUNK_HEADS, heads)
    feats = hidden.shape[1]
    wide = head_n * rows
    hbm = pl.BlockSpec(memory_space=pl.ANY)
    vmem = pl.BlockSpec(memory_space=pltpu.VMEM)
    blk = (heads, DK, DK)
    sem = pltpu.SemaphoreType.DMA
    outs = [jax.ShapeDtypeStruct((tok, width), BF16)] * 4 + [
        jax.ShapeDtypeStruct((tok, feats), BF16)
    ]
    made = pl.pallas_call(
        functools.partial(mix_kernel, seq_n, head_n),
        out_shape=[pltpu.VMEM(o.shape, o.dtype) for o in outs],
        in_specs=[pl.BlockSpec(memory_space=pltpu.HBM)] * 7,
        out_specs=[vmem] * 5,
        scratch_shapes=[
            pltpu.SMEM((levels,), jnp.int32),
            pltpu.VMEM((tok, width), BF16),
            pltpu.VMEM((tok, width), BF16),
            pltpu.VMEM((tok, width), BF16),
            pltpu.VMEM((tok, feats), BF16),
            pltpu.VMEM((feats, wide), BF16),
            pltpu.VMEM((tok, width), BF16),
            pltpu.VMEM((feats, wide), BF16),
            pltpu.VMEM((head_n, rows, tok), F32),
            pltpu.VMEM((head_n - 1, rows, tok), F32),
            pltpu.VMEM((head_n, rows, tok), BF16),
            pltpu.VMEM(blk, F32),
            pltpu.VMEM(blk, BF16),
            pltpu.VMEM(blk, BF16),
            pltpu.VMEM((nb,) + blk, BF16),
            pltpu.VMEM(blk, BF16),
            pltpu.VMEM((nb,) + blk, BF16),
            pltpu.VMEM((nb + 1,) + blk, BF16),
            pltpu.VMEM(blk, BF16),
            pltpu.VMEM(blk, BF16),
            pltpu.VMEM(blk, F32),
            pltpu.VMEM((nb,) + blk, F32),
            pltpu.VMEM(blk, F32),
            pltpu.VMEM(blk, BF16),
            pltpu.VMEM(blk, BF16),
            pltpu.VMEM(blk, BF16),
            pltpu.VMEM((levels,) + blk, F32),
            pltpu.VMEM(blk, BF16),
            pltpu.VMEM((heads, tok, (levels - 1) * DK), BF16),
            sem((7,)),
            sem((head_n - 1,)), sem((head_n - 1,)),
            sem((head_n - 1,)), sem((head_n - 1,)),
            sem((chunks,)), sem((chunks,)),
            sem((nb, chunks)), sem((nb, chunks)),
            sem((nb, chunks)), sem((nb, chunks)),
            sem((chunks,)), sem((chunks,)),
        ],
        compiler_params=pltpu.CompilerParams(
            collective_id=0, has_side_effects=True, vmem_limit_bytes=VMEM_ALL
        ),
    )(level_slot, queries, keys, values, hidden, gate_weight, out_grad)
    return pl.pallas_call(
        hand_over,
        out_shape=outs,
        in_specs=[hbm] * 5,
        out_specs=[hbm] * 5,
        scratch_shapes=[sem((5,))],
        compiler_params=pltpu.CompilerParams(vmem_limit_bytes=4 << 20),
    )(*made)


def solution(mesh):
    both = P("seq", "head")
    return jax.shard_map(
        functools.partial(local, mesh.shape["seq"], mesh.shape["head"]),
        mesh=mesh,
        in_specs=(both, both, both, both, P("head", None), P(), both),
        out_specs=(both,) * 5,
        check_vma=False,
    )
```
